32 devices in a mesh: section: 4 (over y, x), rep: 8 (over z, core).
Axes of the slice: x: 2, y: 2, z: 4, core: 2. Of those that a mesh axis runs over, the one named last changes fastest.
Arguments:
- section_state: float32 [4, 4, 8, 196, 512], P('section', None, 'rep'), may hold values from -6 to 6
- arriving: float32 [2, 4, 8, 196, 512], P(None, None, 'rep'), may hold values from -6 to 6
- first_weight: float32 [4, 1, 9, 512, 128], P('section'), may hold values from -0.1875 to 0.1875
- second_weight: float32 [4, 1, 9, 512, 128], P('section'), may hold values from -0.1875 to 0.1875
Outputs:
- returned: float32 [4, 4, 8, 196, 512], P('section', None, 'rep')
- first_grad: float32 [4, 1, 9, 512, 128], P('section', None, None, 'rep')
- second_grad: float32 [4, 1, 9, 512, 128], P('section', None, None, 'rep')
The draws below stay inside these ranges and needn't reach their ends.
All inputs are finite; a program needn't handle non-finite values.
Results may differ from the reference program's by a relative error of at most 0.00019.
Values sent between devices are 32-bit elements; how exact they have to be, the bound alone decides.
No kernel may reach another device: no remote copies, remote signals or barrier semaphores. Data moves between devices by JAX's collectives and lax.ppermute only.
A program may use at most 128 MiB of HBM per device.

```python
import jax
import jax.numpy as jnp
from jax import lax

C = 512
GROUPS = 4
SIDE = 14
BLOCKS = 1
TICKS = 3
IMAGES = 8
N_SECTION = 4


def shard_levels(key, shape, cuts, smallest, largest):
    def one(position, blocks):
        heights = jax.random.uniform(jax.random.fold_in(jax.random.fold_in(key, 6), position), (blocks,), jnp.float32, smallest / len(cuts), largest / len(cuts))
        return jnp.repeat(jnp.exp(heights), shape[position] // blocks).reshape((-1,) + (1,) * (len(shape) - position - 1))

    level = one(*cuts[0])
    for cut in cuts[1:]:
        level = level * one(*cut)
    return level


def scatter_about(rng, extent, deviation, limit, cuts=(), kind=jnp.bfloat16):
    values = deviation * jax.random.normal(rng, extent, jnp.float32)
    if cuts:
        values = values * shard_levels(rng, extent, cuts, -0.22, 0.18)
    return jnp.clip(values, -limit, limit).astype(kind)


def setup_inputs(seed: int = 0) -> dict:
    streams_of = jax.random.split(jax.random.key(seed), 5)
    section_state = scatter_about(streams_of[0], (N_SECTION, 4, IMAGES, SIDE * SIDE, C), 1.0, 6.0, ((0, 4), (2, 8)), jnp.float32)
    arriving = scatter_about(streams_of[1], (TICKS - 1, 4, IMAGES, SIDE * SIDE, C), 1.0, 6.0, ((2, 8),), jnp.float32)
    first_weight = scatter_about(streams_of[2], (N_SECTION, BLOCKS, 9, C, C // GROUPS), (9 * C // GROUPS) ** -0.5, 0.1875, ((0, 4),), jnp.float32)
    second_weight = scatter_about(streams_of[3], (N_SECTION, BLOCKS, 9, C, C // GROUPS), (9 * C // GROUPS) ** -0.5, 0.1875, ((0, 4),), jnp.float32)
    return {"section_state": section_state, "arriving": arriving, "first_weight": first_weight, "second_weight": second_weight}


def grouped_conv(inputs, weight):
    images, pixels, channels = inputs.shape
    width_group = weight.shape[2]
    groups = channels // width_group
    square = inputs.reshape(images, SIDE, SIDE, channels)
    padded = jnp.pad(square, ((0, 0), (1, 1), (1, 1), (0, 0)))
    windows = jnp.stack([padded[:, row_off:row_off + SIDE, col_off:col_off + SIDE, :].reshape(images, pixels, groups, width_group) for row_off in range(3) for col_off in range(3)])
    kernel = weight.reshape(9, groups, width_group, width_group)
    result = jnp.einsum('tgoi,tbpgi->bpgo', kernel, windows, precision=lax.Precision.HIGHEST, preferred_element_type=jnp.float32)
    return result.reshape(images, pixels, channels)

def branch_fn(inputs, weight):
    return jax.nn.silu(grouped_conv(inputs, weight))

def block_backward(halves, first_filter, second_filter):
    y_one, y_two, e_one, e_two = halves
    act_second, second_back = jax.vjp(branch_fn, y_one, second_filter)
    x_two = y_two - act_second
    act_first, first_back = jax.vjp(branch_fn, x_two, first_filter)
    x_one = y_one - act_first
    into_one, grad_second = second_back(e_two)
    total_one = e_one + into_one
    into_two, grad_first = first_back(total_one)
    return ((x_one, x_two, total_one, e_two + into_two), grad_first, grad_second)

def section_backward(halves, first_section, second_section):
    first_list = [None] * BLOCKS
    second_list = [None] * BLOCKS
    for block_index in range(BLOCKS - 1, -1, -1):
        halves, grad_first, grad_second = block_backward(halves, first_section[block_index], second_section[block_index])
        first_list[block_index] = grad_first
        second_list[block_index] = grad_second
    return (halves, jnp.stack(first_list), jnp.stack(second_list))

def reference(section_state, arriving, first_weight, second_weight):
    sections = section_state.shape[0]
    held = [tuple((section_state[section_index, member] for member in range(4))) for section_index in range(sections)]
    first_total = jnp.zeros(first_weight.shape, jnp.float32)
    second_total = jnp.zeros(second_weight.shape, jnp.float32)
    outcome = held
    for tick_index in range(TICKS):
        outcome = []
        first_parts = []
        second_parts = []
        for section_index in range(sections):
            halves, grad_first, grad_second = section_backward(held[section_index], first_weight[section_index], second_weight[section_index])
            outcome.append(halves)
            first_parts.append(grad_first)
            second_parts.append(grad_second)
        first_total = first_total + jnp.stack(first_parts)
        second_total = second_total + jnp.stack(second_parts)
        if tick_index < TICKS - 1:
            held = outcome[1:] + [tuple((arriving[tick_index, member] for member in range(4)))]
    returned = jnp.stack([jnp.stack(list(halves)) for halves in outcome])
    return (returned, first_total, second_total)
```

```python
import functools
import math

import jax
import jax.numpy as jnp
from jax import lax
from jax.experimental import pallas as pl
from jax.experimental.pallas import tpu as pltpu
from jax.sharding import PartitionSpec as P

F32, BF16 = jnp.float32, jnp.bfloat16
VMEM_LIMIT = 40 * 2**20


def pair(value, axis=1):
    high = value.astype(BF16)
    low = (value - high.astype(F32)).astype(BF16)
    return jnp.concatenate([high, low], axis=axis)


def spread(taps, value, pitch):
    rows = value.shape[0]
    for b in range(3):
        moved = value if b == 1 else pltpu.roll(value, 1 if b == 0 else rows - 1, 0)
        taps[b, pitch : pitch + rows, :] = pair(moved)


def conv(taps, packed, which, rows, pitch, mirrored):
    total = None
    for t in range(9):
        a, b = divmod(8 - t if mirrored else t, 3)
        filters = packed[which, t]
        part = jnp.dot(
            taps[b, a * pitch : a * pitch + rows, :],
            jnp.concatenate([filters, filters], axis=0),
            preferred_element_type=F32,
        )
        total = part if total is None else total + part
    width = total.shape[1] // 2
    return total[:, :width] + total[:, width:]


def filter_grad(turned, taps, depth, pitch, t):
    a, b = divmod(t, 3)
    four = jnp.dot(turned, taps[b, a * pitch : a * pitch + depth, :], preferred_element_type=F32)
    width = four.shape[0] // 2
    return (four[:width, :width] + four[width:, width:]) + (four[:width, width:] + four[width:, :width])


def turn(value, depth):
    rows, width = value.shape
    padded = jnp.concatenate([value, jnp.zeros((depth - rows, width), F32)], axis=0)
    return pair(padded.T, axis=0)


def step_kernel(dims, first, last, *refs):
    side, pitch, groups, width, shares = dims
    rows, pixels = side * pitch, side * side
    depth = -(-rows // 128) * 128
    if first:
        (info, state, first_weight, second_weight, out, packed, grads, held, plane, weights, taps_one, taps_two, taps_error, sems) = refs
    else:
        (info, moved, arriving, packed_in, grads_in, out, grads, held, near, plane, packed, sums, taps_one, taps_two, taps_error, sems) = refs
    group = info[0]

    if first:
        copies = [pltpu.make_async_copy(state, held, sems.at[0])]
        for k, source in enumerate((second_weight, first_weight)):
            lanes = pl.ds(pl.multiple_of(group * width, width), width)
            copies.append(pltpu.make_async_copy(source.at[:, lanes, :], weights.at[k], sems.at[1 + k]))
        for copy in copies:
            copy.start()
    else:
        at_end = info[1] == 1
        from_end = pltpu.make_async_copy(arriving, held, sems.at[0])
        from_near = pltpu.make_async_copy(moved, near, sems.at[0])

        @pl.when(at_end)
        def _():
            from_end.start()

        @pl.when(jnp.logical_not(at_end))
        def _():
            from_near.start()

        copies = [pltpu.make_async_copy(packed_in.at[k], packed.at[k], sems.at[1 + k]) for k in range(4)]
        copies.append(pltpu.make_async_copy(grads_in, sums, sems.at[5]))
        for copy in copies:
            copy.start()

    zeros = jnp.zeros((pitch, 2 * width), BF16)
    for taps in (taps_one, taps_two, taps_error):
        for b in range(3):
            taps[b, 0:pitch, :] = zeros
            for low in range(pitch + rows, taps.shape[1], pitch):
                taps[b, low : low + pitch, :] = zeros
    for member in range(4):
        for r in range(side):
            plane[member, r * pitch + side : (r + 1) * pitch, :] = jnp.zeros((pitch - side, width), F32)

    def take_whole():
        for member in range(4):
            for r in range(side):
                plane[member, r * pitch : r * pitch + side, :] = held[member, pl.ds(r * side * groups + group, side, stride=groups), :]

    def take_near():
        for member in range(4):
            for r in range(side):
                low = member * pixels + r * side
                plane[member, r * pitch : r * pitch + side, :] = near[low : low + side, :]

    if first:
        copies[0].wait()
        take_whole()
    else:
        @pl.when(at_end)
        def _():
            from_end.wait()
            take_whole()

        @pl.when(jnp.logical_not(at_end))
        def _():
            from_near.wait()
            take_near()

    inside = lax.rem(lax.broadcasted_iota(jnp.int32, (rows, width), 0), pitch) < side

    def branch(value):
        gate = 1.0 / (1.0 + jnp.exp(-value))
        return value * gate, gate * (1.0 + value * (1.0 - gate))

    def give(member, value):
        for r in range(side):
            low = member * pixels + r * side
            out[low : low + side, :] = value[r * pitch : r * pitch + side, :]

    def ready(k):
        if first:
            if k < 2:
                copies[1 + k].wait()
                for t in range(9):
                    packed[k, t] = pair(weights[k, t].T)
                    packed[2 + k, t] = pair(weights[k, t])
        else:
            copies[k].wait()

    spread(taps_one, plane[0], pitch)
    ready(0)
    act, slope_two = branch(conv(taps_one, packed, 0, rows, pitch, False))
    x_two = jnp.where(inside, plane[1] - act, 0.0)
    spread(taps_two, x_two, pitch)
    give(1, x_two)
    change_two = jnp.where(inside, plane[3] * slope_two, 0.0)
    spread(taps_error, change_two, pitch)
    ready(2)
    d_one = jnp.where(inside, plane[2] + conv(taps_error, packed, 2, rows, pitch, True), 0.0)
    give(2, d_one)
    ready(1)
    act, slope_one = branch(conv(taps_two, packed, 1, rows, pitch, False))
    give(0, plane[0] - act)
    change_one = jnp.where(inside, d_one * slope_one, 0.0)
    spread(taps_error, change_one, pitch)
    ready(3)
    give(3, plane[3] + conv(taps_error, packed, 3, rows, pitch, True))

    if not first:
        copies[4].wait()
    part = width // shares
    for k, (change, taps) in enumerate(((change_one, taps_two), (change_two, taps_one))):
        turned = turn(change, depth)
        for t in range(9):
            grad = filter_grad(turned, taps, depth, pitch, t)
            if not first:
                grad = grad + sums[k, t]
            if last:
                for h in range(shares):
                    grads[lax.rem(h - info[2] + shares, shares), k, t] = grad[h * part : (h + 1) * part, :]
            else:
                grads[k, t] = grad


def step(dims, info, first, last, operands):
    side, pitch, groups, width, shares = dims
    pixels, rows = side * side, side * pitch
    depth = -(-rows // 128) * 128
    anywhere = pl.BlockSpec(memory_space=pl.ANY)
    whole = pl.BlockSpec(memory_space=pltpu.VMEM)
    packed = (4, 9, width, 2 * width)
    out_shape = [jax.ShapeDtypeStruct((4 * pixels, width), F32)]
    if first:
        out_shape.append(jax.ShapeDtypeStruct(packed, BF16))
    out_shape.append(jax.ShapeDtypeStruct((shares, 2, 9, width // shares, width) if last else (2, 9, width, width), F32))
    held = pltpu.VMEM((4, pixels * groups, width), F32)
    plane = pltpu.VMEM((4, rows, width), F32)
    taps = [pltpu.VMEM((3, 2 * pitch + depth, 2 * width), BF16)] * 3
    if first:
        scratch = [held, plane, pltpu.VMEM((2, 9, width, width), F32)]
    else:
        scratch = [held, pltpu.VMEM((4 * pixels, width), F32), plane, pltpu.VMEM(packed, BF16), pltpu.VMEM((2, 9, width, width), F32)]
    return pl.pallas_call(
        functools.partial(step_kernel, dims, first, last),
        out_shape=out_shape,
        in_specs=[pl.BlockSpec(memory_space=pltpu.SMEM)] + [anywhere] * len(operands),
        out_specs=[whole] * len(out_shape),
        scratch_shapes=scratch + taps + [pltpu.SemaphoreType.DMA((6,))],
        compiler_params=pltpu.CompilerParams(vmem_limit_bytes=VMEM_LIMIT),
        cost_estimate=pl.CostEstimate(flops=6 * 2 * 9 * 4 * rows * width * width, bytes_accessed=6 * 2**20, transcendentals=2 * rows * width),
        name="first_step" if first else "last_step" if last else "step",
    )(info, *operands)


def on_device(section_state, arriving, first_weight, second_weight):
    _, _, _, pixels, channels = section_state.shape
    width = first_weight.shape[-1]
    groups = channels // width
    side = math.isqrt(pixels)
    pitch = -(-(side + 1) // 16) * 16
    sections, reps = lax.axis_size("section"), lax.axis_size("rep")
    shares = reps // groups
    dims = (side, pitch, groups, width, shares)
    ticks = arriving.shape[0] + 1

    state = section_state[0].reshape(4, pixels * groups, width)
    arrivals = arriving.reshape(ticks - 1, 4, pixels * groups, width)
    first_filters, second_filters = first_weight[0, 0], second_weight[0, 0]

    rep = lax.axis_index("rep")
    own, share = rep // shares, rep % shares
    at_end = (lax.axis_index("section") == sections - 1).astype(jnp.int32)
    turns = sorted(range(1, groups), key=lambda k: (-min(k, groups - k), k)) + [0]
    infos = [jnp.stack([(own + k) % groups, at_end, share]).astype(jnp.int32) for k in turns]

    down = [(s, s - 1) for s in range(1, sections)]
    moved, packed, sums, outs = {}, {}, {}, {}

    def run(tick, p):
        first, last = tick == 0, tick == ticks - 1
        if first:
            out, packed[p], sums[p] = step(dims, infos[p], True, last, (state, first_filters, second_filters))
        else:
            out, sums[p] = step(dims, infos[p], False, last, (moved[p], arrivals[tick - 1], packed[p], sums[p]))
        if last:
            outs[p] = out
        else:
            moved[p] = lax.ppermute(out, "section", down)

    def gather_shares(parts):
        total = parts[0]
        for d in range(1, shares):
            total = total + lax.ppermute(parts[d], "rep", [(r, r - r % shares + (r % shares + d) % shares) for r in range(reps)])
        return total

    totals = {}
    order = sorted(((t, p) for t in range(ticks) for p in range(groups)), key=lambda i: (i[1] + 2 * i[0], -i[0]))
    for tick, p in order:
        run(tick, p)
        if tick == ticks - 1:
            total = gather_shares(sums[p])
            k = turns[p]
            if k:
                total = lax.ppermute(total, "rep", [(r, (r + k * shares) % reps) for r in range(reps)])
            totals[p] = total

    grads = functools.reduce(lambda x, y: x + y, [totals[p] for p in range(groups)])
    by_turn = jnp.stack([outs[p].reshape(4, pixels, width) for p in range(groups)], axis=2)
    place = jnp.stack([jnp.int32(turns.index(k)) for k in range(groups)])
    by_group = jnp.take(by_turn, place[(jnp.arange(groups) - own) % groups], axis=2)
    returned = by_group.reshape(1, 4, 1, pixels, channels)
    return (returned, grads[0][None, None], grads[1][None, None])


def solution(mesh):
    return jax.shard_map(
        on_device,
        mesh=mesh,
        in_specs=(
            P("section", None, "rep", None, None),
            P(None, None, "rep", None, None),
            P("section", None, None, None, None),
            P("section", None, None, None, None),
        ),
        out_specs=(
            P("section", None, "rep", None, None),
            P("section", None, None, "rep", None),
            P("section", None, None, "rep", None),
        ),
        check_vma=False,
    )
```

```python
import functools
import math

import jax
import jax.numpy as jnp
from jax import lax
from jax.experimental import pallas as pl
from jax.experimental.pallas import tpu as pltpu
from jax.sharding import PartitionSpec as P

F32, BF16 = jnp.float32, jnp.bfloat16
VMEM_LIMIT = 16 * 2**20
VMEM, HBM, ANY = pltpu.VMEM, pltpu.HBM, pl.ANY


def halves(value):
    high = value.astype(BF16)
    return high, (value - high.astype(F32)).astype(BF16)


def spread(taps, value, pitch):
    rows, width = value.shape
    for b in range(3):
        moved = value if b == 1 else pltpu.roll(value, 1 if b == 0 else rows - 1, 0)
        for k, half in enumerate(halves(moved)):
            low = (3 * k + b) * width
            taps[pitch : pitch + rows, low : low + width] = half


def conv(taps, packed, rows, pitch):
    total = None
    for a in range(3):
        filters = packed[a]
        part = jnp.dot(
            taps[a * pitch : a * pitch + rows, :], jnp.concatenate([filters, filters], axis=0), preferred_element_type=F32
        )
        total = part if total is None else total + part
    width = total.shape[1] // 2
    return total[:, :width] + total[:, width:]


def turn(value, depth):
    rows, width = value.shape
    high, low = halves(jnp.concatenate([value, jnp.zeros((depth - rows, width), F32)], axis=0).T)
    return jnp.concatenate([high, high, low], axis=1)


def step_kernel(dims, k_turn, tick, last, n_after, *refs):
    side, pitch, groups, width, shares = dims
    rows, pixels = side * pitch, side * side
    depth = -(-rows // 128) * 128
    first, lead, final = tick == 0, tick == 0 and n_after == 0, last and k_turn == 0
    refs = list(refs)
    take = lambda n: [refs.pop(0) for _ in range(n)]
    (info,) = take(1)
    if first:
        (state,) = take(1)
        filters = take(2 if lead else 1)
    else:
        moved, arriving, packed, sums_in = take(4)
    others = take(groups - 1) if final else []
    take(n_after)
    (out,) = take(1)
    if first:
        (packed,) = take(1)
        if lead:
            (kept,) = take(1)
    if last:
        grads = take(shares)
    else:
        (sums,) = take(1)
    plane, taps_one, taps_two, taps_error, sems = take(5)
    if lead:
        (weights,) = take(1)
    if not first:
        (held,) = take(1)
    if last:
        (sums,) = take(1)
    if final:
        (whole,) = take(1)

    group = lax.rem(info[0] + k_turn, groups)
    channels = pl.ds(pl.multiple_of(group * width, width), width)
    if lead:
        copies = [pltpu.make_async_copy(f.at[:, channels, :], weights.at[k], sems.at[k]) for k, f in enumerate(filters)]
        copies += [pltpu.make_async_copy(f, kept.at[k], sems.at[2 + k]) for k, f in enumerate(filters)]
        for copy in copies:
            copy.start()
    if not first:
        at_end = info[1] == 1
        from_end = pltpu.make_async_copy(arriving.at[tick - 1], held, sems.at[0])

        @pl.when(at_end)
        def _():
            from_end.start()

    for taps in (taps_one, taps_two, taps_error):
        taps[0:pitch, :] = jnp.zeros((pitch, 6 * width), BF16)
        low = pitch + rows
        taps[low:, :] = jnp.zeros((taps.shape[0] - low, 6 * width), BF16)
    for member in range(4):
        for r in range(side):
            plane[member, r * pitch + side : (r + 1) * pitch, :] = jnp.zeros((pitch - side, width), F32)

    def take_whole(source):
        for member in range(4):
            for r in range(side):
                plane[member, r * pitch : r * pitch + side, :] = source[
                    member, pl.ds(r * side * groups + group, side, stride=groups), :
                ]

    if first:
        take_whole(state)
    else:

        @pl.when(at_end)
        def _():
            from_end.wait()
            take_whole(held)

        @pl.when(jnp.logical_not(at_end))
        def _():
            for member in range(4):
                for r in range(side):
                    low = member * pixels + r * side
                    plane[member, r * pitch : r * pitch + side, :] = moved[low : low + side, :]

    inside = lax.rem(lax.broadcasted_iota(jnp.int32, (rows, width), 0), pitch) < side

    def branch(value):
        gate = 1.0 / (1.0 + jnp.exp(-value))
        return value * gate, gate * (1.0 + value * (1.0 - gate))

    leaving = []

    def give(member, value):
        if final:
            for slot, other in enumerate(others):
                theirs = lax.rem(info[0] + others_turns(groups)[slot], groups)
                whole[member, pl.ds(theirs, pixels, stride=groups), :] = other[member * pixels : (member + 1) * pixels, :]
        for r in range(side):
            piece = value[r * pitch : r * pitch + side, :]
            if final:
                whole[member, pl.ds(r * side * groups + group, side, stride=groups), :] = piece
            else:
                low = member * pixels + r * side
                out[low : low + side, :] = piece
        if final:
            copy = pltpu.make_async_copy(whole.at[member], out.at[member], sems.at[1 + member])
            copy.start()
            leaving.append(copy)

    def pack(k):
        for t in range(9):
            if lead:
                tap, mirror = weights[k, t], weights[k, 8 - t]
            else:
                tap, mirror = filters[0][k, t, channels, :], filters[0][k, 8 - t, channels, :]
            a, b = divmod(t, 3)
            packed[k, a, b * width : (b + 1) * width, :] = jnp.concatenate(halves(tap.T), axis=1)
            packed[2 + k, a, b * width : (b + 1) * width, :] = jnp.concatenate(halves(mirror), axis=1)

    spread(taps_one, plane[0], pitch)
    if first:
        if lead:
            copies[1].wait()
        pack(1)
    act, slope_two = branch(conv(taps_one, packed.at[1], rows, pitch))
    x_two = jnp.where(inside, plane[1] - act, 0.0)
    spread(taps_two, x_two, pitch)
    give(1, x_two)
    change_two = jnp.where(inside, plane[3] * slope_two, 0.0)
    spread(taps_error, change_two, pitch)
    d_one = jnp.where(inside, plane[2] + conv(taps_error, packed.at[3], rows, pitch), 0.0)
    give(2, d_one)
    if first:
        if lead:
            copies[0].wait()
        pack(0)
    act, slope_one = branch(conv(taps_two, packed.at[0], rows, pitch))
    give(0, plane[0] - act)
    change_one = jnp.where(inside, d_one * slope_one, 0.0)
    spread(taps_error, change_one, pitch)
    give(3, plane[3] + conv(taps_error, packed.at[2], rows, pitch))

    for k, (change, taps) in enumerate(((change_one, taps_two), (change_two, taps_one))):
        turned = turn(change, depth)
        for a in range(3):
            high = taps[a * pitch : a * pitch + depth, : 3 * width]
            low = taps[a * pitch : a * pitch + depth, 3 * width :]
            grad = jnp.dot(turned, jnp.concatenate([high, low, high], axis=0), preferred_element_type=F32)
            for b in range(3):
                tap = grad[:, b * width : (b + 1) * width]
                sums[k, 3 * a + b] = tap if first else tap + sums_in[k, 3 * a + b]
    if last:
        part = width // shares
        for d in range(shares):
            low = pl.multiple_of(lax.rem(info[2] + d, shares) * part, part)
            grads[d][...] = sums[:, :, pl.ds(low, part), :]
    if lead:
        copies[2].wait()
        copies[3].wait()
    for copy in leaving:
        copy.wait()


def others_turns(groups):
    return sorted(range(1, groups), key=lambda k: (-min(k, groups - k), k))


def step(dims, k_turn, tick, last, info, operands, after):
    side, pitch, groups, width, shares = dims
    pixels, rows = side * side, side * pitch
    depth = -(-rows // 128) * 128
    first, lead, final = tick == 0, tick == 0 and not after, last and k_turn == 0
    in_vmem = pl.BlockSpec(memory_space=VMEM)
    anywhere = pl.BlockSpec(memory_space=ANY)

    def local(array):
        return pltpu.with_memory_space_constraint(array, VMEM)

    def far(array):
        return pltpu.with_memory_space_constraint(array, HBM)

    sums = (2, 9, width, width)
    specs, args = [pl.BlockSpec(memory_space=pltpu.SMEM)], [info]

    def give(array, where, spec):
        args.append(where(array))
        specs.append(spec)

    if first:
        state, *filters = operands
        give(state, local, in_vmem)
        for f in filters:
            give(f, far if lead else local, anywhere if lead else in_vmem)
    else:
        moved, arriving, packed, before, *others = operands
        give(moved, lambda x: x, in_vmem)
        give(arriving, far, anywhere)
        for x in (packed, before, *others):
            give(x, local, in_vmem)
    for x in after:
        give(x, lambda x: x, anywhere)

    if final:
        out_shape, out_specs = [jax.ShapeDtypeStruct((4, pixels * groups, width), F32)], [anywhere]
    else:
        out_shape, out_specs = [VMEM((4 * pixels, width), F32)], [in_vmem]
    if first:
        out_shape.append(VMEM((4, 3, 3 * width, 2 * width), BF16))
        if lead:
            out_shape.append(VMEM((2, 9, groups * width, width), F32))
    if last:
        out_shape += [VMEM((2, 9, width // shares, width), F32)] * shares
    else:
        out_shape.append(VMEM(sums, F32))
    out_specs += [in_vmem] * (len(out_shape) - 1)

    scratch = [VMEM((4, rows, width), F32)] + [VMEM((2 * pitch + depth, 6 * width), BF16)] * 3 + [pltpu.SemaphoreType.DMA((6,))]
    if lead:
        scratch.append(VMEM(sums, F32))
    if not first:
        scratch.append(VMEM((4, pixels * groups, width), F32))
    if last:
        scratch.append(VMEM(sums, F32))
    if final:
        scratch.append(VMEM((4, pixels * groups, width), F32))
    return pl.pallas_call(
        functools.partial(step_kernel, dims, k_turn, tick, last, len(after)),
        out_shape=out_shape,
        in_specs=specs,
        out_specs=out_specs,
        scratch_shapes=scratch,
        compiler_params=pltpu.CompilerParams(vmem_limit_bytes=VMEM_LIMIT),
        cost_estimate=pl.CostEstimate(
            flops=6 * 2 * 9 * 4 * rows * width * width, bytes_accessed=6 * 2**20, transcendentals=2 * rows * width
        ),
        name=f"tick_{tick}_turn_{k_turn}",
    )(*args)


def add_kernel(n, *refs):
    for k, out in enumerate(refs[n:]):
        out[...] = functools.reduce(lambda x, y: x + y, [ref[k] for ref in refs[:n]])


def on_device(section_state, arriving, first_weight, second_weight):
    _, _, _, pixels, channels = section_state.shape
    width = first_weight.shape[-1]
    groups = channels // width
    side = math.isqrt(pixels)
    pitch = -(-(side + 1) // 16) * 16
    sections, reps = lax.axis_size("section"), lax.axis_size("rep")
    shares = reps // groups
    dims = (side, pitch, groups, width, shares)
    ticks = arriving.shape[0] + 1

    state = section_state[0].reshape(4, pixels * groups, width)
    arrivals = arriving.reshape(ticks - 1, 4, pixels * groups, width)
    filters = (first_weight[0, 0], second_weight[0, 0])

    rep = lax.axis_index("rep")
    at_end = lax.axis_index("section") == sections - 1
    info = jnp.stack([rep // shares, at_end.astype(jnp.int32), rep % shares]).astype(jnp.int32)

    turns = others_turns(groups) + [0]
    down = [(s, s - 1) for s in range(1, sections)]
    moved, packed, sums, outs, totals, waiting = {}, {}, {}, {}, {}, {}

    def gather_shares(parts):
        total = parts[0]
        for d in range(1, shares):
            total = total + lax.ppermute(parts[d], "rep", [(r, r - r % shares + (r % shares + d) % shares) for r in range(reps)])
        return total

    order = sorted(((t, p) for t in range(ticks) for p in range(groups)), key=lambda i: (i[1] + 2 * i[0], -i[0]))
    for n, (tick, p) in enumerate(order):
        k, last = turns[p], tick == ticks - 1
        after = waiting.pop(n, [])
        if tick == 0:
            results = list(step(dims, k, tick, last, info, (state, *filters), after))
            if n == 0:
                filters = (results.pop(2),)
            out, packed[p], *grads = results
        else:
            others = [outs[o] for o in range(p)] if last and k == 0 else []
            out, *grads = step(dims, k, tick, last, info, (moved[p], arrivals, packed[p], sums[p], *others), after)
        waiting.setdefault(n + 1, []).append(out)
        if not last:
            sums[p] = grads[0]
            moved[p] = lax.ppermute(out, "section", down)
            continue
        outs[p] = out
        if k:
            total = gather_shares(grads)
            waiting.setdefault(min(n + 2, len(order) - 1), []).append(total)
            totals[p] = [lax.ppermute(total, "rep", [(r, (r + k * shares) % reps) for r in range(reps)])]
        else:
            totals[p] = [grads[0]] + [
                lax.ppermute(grads[d], "rep", [(r, r - r % shares + (r % shares + d) % shares) for r in range(reps)])
                for d in range(1, shares)
            ]

    terms = [x for p in range(groups) for x in totals[p]]
    part = terms[0].shape[1:]
    first_grad, second_grad = pl.pallas_call(
        functools.partial(add_kernel, len(terms)),
        out_shape=[jax.ShapeDtypeStruct(part, F32)] * 2,
        in_specs=[pl.BlockSpec(memory_space=VMEM)] * len(terms),
        out_specs=[pl.BlockSpec(memory_space=VMEM)] * 2,
        compiler_params=pltpu.CompilerParams(vmem_limit_bytes=VMEM_LIMIT),
        name="add_gradients",
    )(*terms)
    returned = outs[groups - 1].reshape(1, 4, 1, pixels, channels)
    return (returned, first_grad[None, None], second_grad[None, None])


def solution(mesh):
    return jax.shard_map(
        on_device,
        mesh=mesh,
        in_specs=(
            P("section", None, "rep", None, None),
            P(None, None, "rep", None, None),
            P("section", None, None, None, None),
            P("section", None, None, None, None),
        ),
        out_specs=(
            P("section", None, "rep", None, None),
            P("section", None, None, "rep", None),
            P("section", None, None, "rep", None),
        ),
        check_vma=False,
    )
```

```python
import functools
import math

import jax
import jax.numpy as jnp
from jax import lax
from jax.experimental import pallas as pl
from jax.experimental.pallas import tpu as pltpu
from jax.sharding import PartitionSpec as P

F32, BF16 = jnp.float32, jnp.bfloat16
VMEM_LIMIT = 16 * 2**20
VMEM, HBM, ANY = pltpu.VMEM, pltpu.HBM, pl.ANY
PLAN = {'step': {1: 1000000000, 5: 1000000000, 6: 10000000000, 7: 10000000000, 8: 1000000000, 9: 10000000000, 10: 100000000000}, 'add': {1: 100000000000, 2: 10000000000}, 'need': {0: 8, 1: 9, 2: 11}, 'wait': {0: [2]}, 'sum': 100000000000, 'last': 100000000000, 'zneed': {}}


def halves(value):
    high = value.astype(BF16)
    return high, (value - high.astype(F32)).astype(BF16)


def spread(taps, value, pitch):
    rows, width = value.shape
    for b in range(3):
        moved = value if b == 1 else pltpu.roll(value, 1 if b == 0 else rows - 1, 0)
        for k, half in enumerate(halves(moved)):
            low = (3 * k + b) * width
            taps[pitch : pitch + rows, low : low + width] = half


def conv(taps, packed, rows, pitch):
    total = None
    for a in range(3):
        filters = packed[a]
        part = jnp.dot(
            taps[a * pitch : a * pitch + rows, :], jnp.concatenate([filters, filters], axis=0), preferred_element_type=F32
        )
        total = part if total is None else total + part
    width = total.shape[1] // 2
    return total[:, :width] + total[:, width:]


def turn(value, depth):
    rows, width = value.shape
    high, low = halves(jnp.concatenate([value, jnp.zeros((depth - rows, width), F32)], axis=0).T)
    return jnp.concatenate([high, high, low], axis=1)


def step_kernel(dims, k_turn, tick, last, n_after, *refs):
    side, pitch, groups, width, shares = dims
    rows, pixels = side * pitch, side * side
    depth = -(-rows // 128) * 128
    first, lead, final = tick == 0, tick == 0 and n_after == 0, last and k_turn == 0
    refs = list(refs)
    take = lambda n: [refs.pop(0) for _ in range(n)]
    (info,) = take(1)
    if first:
        (state,) = take(1)
        filters = take(2 if lead else 1)
    else:
        moved, arriving, packed, sums_in = take(4)
    others = take(groups - 1) if final else []
    take(n_after)
    (out,) = take(1)
    if first:
        (packed,) = take(1)
        if lead:
            (kept,) = take(1)
    if last:
        grads = take(1 + 2 * (shares - 1) if final else 1)
    else:
        (sums,) = take(1)
    plane, taps_one, taps_two, taps_error, sems = take(5)
    if lead:
        (weights,) = take(1)
    if last:
        (sums,) = take(1)
    if final:
        (whole,) = take(1)

    group = info[0] ^ k_turn
    channels = pl.ds(pl.multiple_of(group * width, width), width)
    if lead:
        copies = [pltpu.make_async_copy(f.at[:, channels, :], weights.at[k], sems.at[k]) for k, f in enumerate(filters)]
        copies += [pltpu.make_async_copy(f, kept.at[k], sems.at[2 + k]) for k, f in enumerate(filters)]
        for copy in copies:
            copy.start()
    if not first:
        at_end = info[1] == 1

    for taps in (taps_one, taps_two, taps_error):
        taps[0:pitch, :] = jnp.zeros((pitch, 6 * width), BF16)
        low = pitch + rows
        taps[low:, :] = jnp.zeros((taps.shape[0] - low, 6 * width), BF16)
    for member in range(4):
        for r in range(side):
            plane[member, r * pitch + side : (r + 1) * pitch, :] = jnp.zeros((pitch - side, width), F32)

    def take_whole(source):
        for member in range(4):
            for r in range(side):
                plane[member, r * pitch : r * pitch + side, :] = source[
                    member, pl.ds(r * side * groups + group, side, stride=groups), :
                ]

    if first:
        take_whole(state)
    else:

        @pl.when(at_end)
        def _():
            take_whole(arriving.at[tick - 1])

        @pl.when(jnp.logical_not(at_end))
        def _():
            for member in range(4):
                for r in range(side):
                    low = member * pixels + r * side
                    plane[member, r * pitch : r * pitch + side, :] = moved[low : low + side, :]

    inside = lax.rem(lax.broadcasted_iota(jnp.int32, (rows, width), 0), pitch) < side

    def branch(value):
        gate = 1.0 / (1.0 + jnp.exp(-value))
        return value * gate, gate * (1.0 + value * (1.0 - gate))

    leaving = []

    def give(member, value):
        if final:
            for slot, other in enumerate(others):
                theirs = info[0] ^ (groups - 1 - slot)
                whole[member, pl.ds(theirs, pixels, stride=groups), :] = other[member * pixels : (member + 1) * pixels, :]
        for r in range(side):
            piece = value[r * pitch : r * pitch + side, :]
            if final:
                whole[member, pl.ds(r * side * groups + group, side, stride=groups), :] = piece
            else:
                low = member * pixels + r * side
                out[low : low + side, :] = piece
        if final:
            copy = pltpu.make_async_copy(whole.at[member], out.at[member], sems.at[1 + member])
            copy.start()
            leaving.append(copy)

    def pack(k):
        for t in range(9):
            if lead:
                tap, mirror = weights[k, t], weights[k, 8 - t]
            else:
                tap, mirror = filters[0][k, t, channels, :], filters[0][k, 8 - t, channels, :]
            a, b = divmod(t, 3)
            packed[k, a, b * width : (b + 1) * width, :] = jnp.concatenate(halves(tap.T), axis=1)
            packed[2 + k, a, b * width : (b + 1) * width, :] = jnp.concatenate(halves(mirror), axis=1)

    spread(taps_one, plane[0], pitch)
    if first:
        if lead:
            copies[1].wait()
        pack(1)
    act, slope_two = branch(conv(taps_one, packed.at[1], rows, pitch))
    x_two = jnp.where(inside, plane[1] - act, 0.0)
    spread(taps_two, x_two, pitch)
    give(1, x_two)
    change_two = jnp.where(inside, plane[3] * slope_two, 0.0)
    spread(taps_error, change_two, pitch)
    d_one = jnp.where(inside, plane[2] + conv(taps_error, packed.at[3], rows, pitch), 0.0)
    give(2, d_one)
    if first:
        if lead:
            copies[0].wait()
        pack(0)
    act, slope_one = branch(conv(taps_two, packed.at[0], rows, pitch))
    give(0, plane[0] - act)
    change_one = jnp.where(inside, d_one * slope_one, 0.0)
    spread(taps_error, change_one, pitch)
    give(3, plane[3] + conv(taps_error, packed.at[2], rows, pitch))

    for k, (change, taps) in enumerate(((change_one, taps_two), (change_two, taps_one))):
        turned = turn(change, depth)
        for a in range(3):
            high = taps[a * pitch : a * pitch + depth, : 3 * width]
            low = taps[a * pitch : a * pitch + depth, 3 * width :]
            grad = jnp.dot(turned, jnp.concatenate([high, low, high], axis=0), preferred_element_type=F32)
            for b in range(3):
                tap = grad[:, b * width : (b + 1) * width]
                sums[k, 3 * a + b] = tap if first else tap + sums_in[k, 3 * a + b]
    if last:
        part = width // shares
        for d in range(shares):
            if final:
                rows_of = pl.ds(pl.multiple_of(lax.rem(info[2] + d, shares) * part, part), part)
                if d == 0:
                    grads[0][...] = sums[:, :, rows_of, :]
                else:
                    for k in range(2):
                        grads[2 * d - 1 + k][...] = sums[k, :, rows_of, :]
            else:
                grads[0][d] = sums[:, :, d * part : (d + 1) * part, :]
    if lead:
        copies[2].wait()
        copies[3].wait()
    for copy in leaving:
        copy.wait()


def step(dims, k_turn, tick, last, info, operands, after, effort):
    side, pitch, groups, width, shares = dims
    pixels, rows = side * side, side * pitch
    depth = -(-rows // 128) * 128
    first, lead, final = tick == 0, tick == 0 and not after, last and k_turn == 0
    in_vmem = pl.BlockSpec(memory_space=VMEM)
    anywhere = pl.BlockSpec(memory_space=ANY)

    def local(array):
        return pltpu.with_memory_space_constraint(array, VMEM)

    def far(array):
        return pltpu.with_memory_space_constraint(array, HBM)

    sums = (2, 9, width, width)
    specs, args = [pl.BlockSpec(memory_space=pltpu.SMEM)], [info]

    def give(array, where, spec):
        args.append(where(array))
        specs.append(spec)

    if first:
        state, *filters = operands
        give(state, local, in_vmem)
        for f in filters:
            give(f, far if lead else local, anywhere if lead else in_vmem)
    else:
        moved, arriving, packed, before, *others = operands
        give(moved, lambda x: x, in_vmem)
        give(arriving, local, in_vmem)
        for x in (packed, before, *others):
            give(x, local, in_vmem)
    for x in after:
        give(x, lambda x: x, anywhere)

    if final:
        out_shape, out_specs = [jax.ShapeDtypeStruct((4, pixels * groups, width), F32)], [anywhere]
    else:
        out_shape, out_specs = [VMEM((4 * pixels, width), F32)], [in_vmem]
    if first:
        out_shape.append(VMEM((4, 3, 3 * width, 2 * width), BF16))
        if lead:
            out_shape.append(VMEM((2, 9, groups * width, width), F32))
    if last:
        part = (2, 9, width // shares, width)
        out_shape += [VMEM(part, F32)] + [VMEM(part[1:], F32)] * (2 * (shares - 1)) if final else [VMEM((shares, *part), F32)]
    else:
        out_shape.append(VMEM(sums, F32))
    out_specs += [in_vmem] * (len(out_shape) - 1)

    scratch = [VMEM((4, rows, width), F32)] + [VMEM((2 * pitch + depth, 6 * width), BF16)] * 3 + [pltpu.SemaphoreType.DMA((6,))]
    if lead:
        scratch.append(VMEM(sums, F32))
    if last:
        scratch.append(VMEM(sums, F32))
    if final:
        scratch.append(VMEM((4, pixels * groups, width), F32))
    return pl.pallas_call(
        functools.partial(step_kernel, dims, k_turn, tick, last, len(after)),
        out_shape=out_shape,
        in_specs=specs,
        out_specs=out_specs,
        scratch_shapes=scratch,
        compiler_params=pltpu.CompilerParams(vmem_limit_bytes=VMEM_LIMIT),
        cost_estimate=pl.CostEstimate(flops=effort, bytes_accessed=1, transcendentals=0),
        name=f"tick_{tick}_turn_{k_turn}",
    )(*args)


def add_kernel(n_terms, n_parts, n_after, *refs):
    outs = refs[n_terms + n_parts + n_after :]
    for k in range(2):
        terms = [ref[k] for ref in refs[:n_terms]] + [ref[...] for ref in refs[n_terms + k : n_terms + n_parts : 2]]
        total = functools.reduce(lambda x, y: x + y, terms)
        if len(outs) > 1:
            outs[k][...] = total
        else:
            outs[0][k] = total


def stack_kernel(n_terms, n_after, stacked, *refs):
    terms = [stacked[n] for n in range(stacked.shape[0])] + [ref[...] for ref in refs[:n_terms]]
    refs[n_terms + n_after][...] = functools.reduce(lambda x, y: x + y, terms)


def add(kernel, arrays, after, effort, out, name):
    in_vmem = pl.BlockSpec(memory_space=VMEM)
    return pl.pallas_call(
        kernel,
        out_shape=out,
        in_specs=[in_vmem] * len(arrays) + [pl.BlockSpec(memory_space=ANY)] * len(after),
        out_specs=[in_vmem] * len(out) if isinstance(out, list) else in_vmem,
        compiler_params=pltpu.CompilerParams(vmem_limit_bytes=VMEM_LIMIT),
        cost_estimate=pl.CostEstimate(flops=effort, bytes_accessed=1, transcendentals=0),
        name=name,
    )(*arrays, *after)


def on_device(section_state, arriving, first_weight, second_weight):
    _, _, _, pixels, channels = section_state.shape
    width = first_weight.shape[-1]
    groups = channels // width
    side = math.isqrt(pixels)
    pitch = -(-(side + 1) // 16) * 16
    sections, reps = lax.axis_size("section"), lax.axis_size("rep")
    shares = reps // groups
    dims = (side, pitch, groups, width, shares)
    ticks = arriving.shape[0] + 1

    state = section_state[0].reshape(4, pixels * groups, width)
    arrivals = arriving.reshape(ticks - 1, 4, pixels * groups, width)
    filters = (first_weight[0, 0], second_weight[0, 0])

    rep = lax.axis_index("rep")
    at_end = lax.axis_index("section") == sections - 1
    info = jnp.stack([rep // shares, at_end.astype(jnp.int32), rep % shares]).astype(jnp.int32)

    turns = list(range(groups - 1, -1, -1))
    down = [(s, s - 1) for s in range(1, sections)]
    moved, packed, sums, outs, totals, waiting, mine = {}, {}, {}, {}, {}, {}, None

    def swap(part, d):
        return lax.ppermute(part, "rep", [(r, r - r % shares + (r % shares + d) % shares) for r in range(reps)])

    order = sorted(((t, p) for t in range(ticks) for p in range(groups)), key=lambda i: (i[1] + 2 * i[0], -i[0]))
    for n, (tick, p) in enumerate(order):
        k, last = turns[p], tick == ticks - 1
        after = waiting.pop(n, [])
        effort = PLAN["step"].get(n, 1)
        if tick == 0:
            results = list(step(dims, k, tick, last, info, (state, *filters), after, effort))
            if n == 0:
                filters = (results.pop(2),)
            out, packed[p], *grads = results
        else:
            others = [outs[o] for o in range(p)] if last and k == 0 else []
            out, *grads = step(dims, k, tick, last, info, (moved[p], arrivals, packed[p], sums[p], *others), after, effort)
        waiting.setdefault(n + 1, []).append(out)
        if not last:
            sums[p] = grads[0]
            moved[p] = lax.ppermute(out, "section", down)
            continue
        outs[p] = out
        if k:
            chips = [list(range(low, low + shares)) for low in range(0, reps, shares)]
            stacked = lax.all_to_all(grads[0], "rep", 0, 0, axis_index_groups=chips)
            after = [moved[q] for q in PLAN["wait"].get(p, [])]
            out = VMEM(stacked.shape[1:], F32)
            partial = [totals.pop(0)] if p == 1 else []
            total = add(functools.partial(stack_kernel, len(partial), len(after)), [stacked, *partial], after, PLAN["add"].get(p, 1), out, f"add_turn_{k}")
            if p in PLAN["need"]:
                waiting.setdefault(PLAN["need"][p], []).append(total)
            mask = 1 if p == 0 else k
            totals[p] = lax.ppermute(total, "rep", [(r, (r // shares ^ mask) * shares + r % shares) for r in range(reps)])
            if p in PLAN["zneed"]:
                waiting.setdefault(PLAN["zneed"][p], []).append(totals[p])
        else:
            mine, swapped = grads[0], [swap(x, 1 + h // 2) for h, x in enumerate(grads[1:])]

    arrived = [mine, *totals.values()]
    out = VMEM(mine.shape, F32)
    kept = add(functools.partial(add_kernel, len(arrived), 0, 0), arrived, [], PLAN["sum"], out, "add_arrived")
    out = [jax.ShapeDtypeStruct(mine.shape[1:], F32)] * 2
    first_grad, second_grad = add(
        functools.partial(add_kernel, 1, len(swapped), 0), [kept, *swapped], [], PLAN["last"], out, "add_last"
    )
    returned = outs[groups - 1].reshape(1, 4, 1, pixels, channels)
    return (returned, first_grad[None, None], second_grad[None, None])


def solution(mesh):
    return jax.shard_map(
        on_device,
        mesh=mesh,
        in_specs=(
            P("section", None, "rep", None, None),
            P(None, None, "rep", None, None),
            P("section", None, None, None, None),
            P("section", None, None, None, None),
        ),
        out_specs=(
            P("section", None, "rep", None, None),
            P("section", None, None, "rep", None),
            P("section", None, None, "rep", None),
        ),
        check_vma=False,
    )
```

```python
import functools
import math

import jax
import jax.numpy as jnp
from jax import lax
from jax.experimental import pallas as pl
from jax.experimental.pallas import tpu as pltpu
from jax.sharding import PartitionSpec as P

F32, BF16 = jnp.float32, jnp.bfloat16
VMEM_LIMIT = 8 * 2**20
VMEM, HBM, ANY = pltpu.VMEM, pltpu.HBM, pl.ANY
PLAN = {'step': {(1, 0): 10000000000, (1, 1): 100000000000, (1, 2): 10000000000, (2, 1): 1000000000, (1, 3): 10000000000}, 'add': {0: 1000000000}, 'need': {0: (1, 2), 2: (2, 3), 1: (2, 2)}, 'wait': {0: [2]}, 'znd': {}, 'swap': {3: 2, 0: 0, 1: 1, 2: 2}, 'sum': 10000000000, 'last': 1, 'order': ((0, 0), (0, 1), (1, 0), (0, 2), (1, 1), (0, 3), (2, 0), (1, 2), (2, 1), (1, 3), (2, 2), (2, 3))}


def halves(value):
    high = value.astype(BF16)
    return high, (value - high.astype(F32)).astype(BF16)


def spread(taps, value, pitch, shifted):
    rows, width = value.shape
    shifted[8 : 8 + rows, :] = value
    for b in range(3):
        moved = value if b == 1 else shifted[7 + b : 7 + b + rows, :]
        for k, half in enumerate(halves(moved)):
            low = (3 * k + b) * width
            taps[pitch : pitch + rows, low : low + width] = half


def conv(taps, packed, rows, pitch):
    total = None
    for a in range(3):
        filters = packed[a]
        part = jnp.dot(
            taps[a * pitch : a * pitch + rows, :], jnp.concatenate([filters, filters], axis=0), preferred_element_type=F32
        )
        total = part if total is None else total + part
    width = total.shape[1] // 2
    return total[:, :width] + total[:, width:]


def turn(value, depth):
    rows, width = value.shape
    high, low = halves(jnp.concatenate([value, jnp.zeros((depth - rows, width), F32)], axis=0).T)
    return jnp.concatenate([high, high, low], axis=1)


def step_kernel(dims, k_turn, tick, last, n_after, pieces, *refs):
    side, pitch, groups, width, shares = dims
    rows, pixels = side * pitch, side * side
    depth = -(-rows // 128) * 128
    first, lead, final = tick == 0, tick == 0 and n_after == 0, last and k_turn == 0
    refs = list(refs)
    take = lambda n: [refs.pop(0) for _ in range(n)]
    (info,) = take(1)
    if first:
        (state,) = take(1)
        filters = take(2 if lead else 1)
    else:
        moved, arriving, packed, sums_in = take(4)
    others = take(groups - 1) if final else []
    take(n_after)
    (out,) = take(1)
    if first:
        (packed,) = take(1)
        if lead:
            kept, kept_state = take(2)
    if last:
        grads = take(1 + pieces * (shares - 1))
    else:
        (sums,) = take(1)
    plane, taps_one, taps_two, taps_error, sems, shifted = take(6)
    shifted[0:8, :] = jnp.zeros((8, width), F32)
    shifted[8 + rows :, :] = jnp.zeros((8, width), F32)
    if lead:
        (weights,) = take(1)
    if last:
        (sums,) = take(1)
    if final:
        (whole,) = take(1)

    group = info[0] ^ k_turn
    channels = pl.ds(pl.multiple_of(group * width, width), width)
    if lead:
        copies = [pltpu.make_async_copy(f.at[:, channels, :], weights.at[k], sems.at[k]) for k, f in enumerate(filters)]
        copies += [pltpu.make_async_copy(f, kept.at[k], sems.at[2 + k]) for k, f in enumerate(filters)]
        from_state = pltpu.make_async_copy(state, kept_state, sems.at[4])
        from_state.start()
        for copy in copies:
            copy.start()
    if not first:
        at_end = info[1] == 1
    for taps in (taps_one, taps_two, taps_error):
        taps[0:pitch, :] = jnp.zeros((pitch, 6 * width), BF16)
        low = pitch + rows
        taps[low:, :] = jnp.zeros((taps.shape[0] - low, 6 * width), BF16)
    for member in range(4):
        for r in range(side):
            plane[member, r * pitch + side : (r + 1) * pitch, :] = jnp.zeros((pitch - side, width), F32)

    if lead:
        from_state.wait()
        state = kept_state
    for member in range(4):
        for r in range(side):
            low = member * pixels + r * side
            strided = pl.ds(r * side * groups + group, side, stride=groups)
            if first:
                row = state[member, strided, :]
            else:
                row = jnp.where(at_end, arriving[tick - 1, member, strided, :], moved[low : low + side, :])
            plane[member, r * pitch : r * pitch + side, :] = row

    inside = lax.rem(lax.broadcasted_iota(jnp.int32, (rows, width), 0), pitch) < side

    def branch(value):
        gate = 1.0 / (1.0 + jnp.exp(-value))
        return value * gate, gate * (1.0 + value * (1.0 - gate))

    leaving = []

    def give(member, value):
        if final:
            for slot, other in enumerate(others):
                theirs = info[0] ^ (groups - 1 - slot)
                whole[member, pl.ds(theirs, pixels, stride=groups), :] = other[member * pixels : (member + 1) * pixels, :]
        for r in range(side):
            piece = value[r * pitch : r * pitch + side, :]
            if final:
                whole[member, pl.ds(r * side * groups + group, side, stride=groups), :] = piece
            else:
                low = member * pixels + r * side
                out[low : low + side, :] = piece
        if final:
            copy = pltpu.make_async_copy(whole.at[member], out.at[member], sems.at[1 + member])
            copy.start()
            leaving.append(copy)

    def pack(k):
        for t in range(9):
            if lead:
                tap, mirror = weights[k, t], weights[k, 8 - t]
            else:
                tap, mirror = filters[0][k, t, channels, :], filters[0][k, 8 - t, channels, :]
            a, b = divmod(t, 3)
            packed[k, a, b * width : (b + 1) * width, :] = jnp.concatenate(halves(tap.T), axis=1)
            packed[2 + k, a, b * width : (b + 1) * width, :] = jnp.concatenate(halves(mirror), axis=1)

    def filter_grads(k, change, taps):
        turned = turn(change, depth)
        for a in range(3):
            high = taps[a * pitch : a * pitch + depth, : 3 * width]
            low = taps[a * pitch : a * pitch + depth, 3 * width :]
            grad = jnp.dot(turned, jnp.concatenate([high, low, high], axis=0), preferred_element_type=F32)
            for b in range(3):
                tap = grad[:, b * width : (b + 1) * width]
                sums[k, 3 * a + b] = tap if first else tap + sums_in[k, 3 * a + b]

    spread(taps_one, plane[0], pitch, shifted)
    if first:
        if lead:
            copies[1].wait()
        pack(1)
    act, slope_two = branch(conv(taps_one, packed.at[1], rows, pitch))
    x_two = jnp.where(inside, plane[1] - act, 0.0)
    spread(taps_two, x_two, pitch, shifted)
    give(1, x_two)
    change_two = jnp.where(inside, plane[3] * slope_two, 0.0)
    spread(taps_error, change_two, pitch, shifted)
    if first:
        if lead:
            copies[0].wait()
        pack(0)
    raw_one = conv(taps_two, packed.at[0], rows, pitch)
    raw_error = conv(taps_error, packed.at[3], rows, pitch)
    act, slope_one = branch(raw_one)
    give(0, plane[0] - act)
    d_one = jnp.where(inside, plane[2] + raw_error, 0.0)
    give(2, d_one)
    filter_grads(1, change_two, taps_one)
    change_one = jnp.where(inside, d_one * slope_one, 0.0)
    spread(taps_error, change_one, pitch, shifted)
    give(3, plane[3] + conv(taps_error, packed.at[2], rows, pitch))

    filter_grads(0, change_one, taps_two)
    if last:
        part = width // shares
        for d in range(shares):
            rows_of = pl.ds(pl.multiple_of(lax.rem(info[2] + d, shares) * part, part), part)
            if pieces == 0:
                grads[0][d] = sums[:, :, d * part : (d + 1) * part, :]
            elif d == 0 or pieces == 1:
                grads[d][...] = sums[:, :, rows_of, :]
            else:
                for k in range(2):
                    grads[2 * d - 1 + k][...] = sums[k, :, rows_of, :]
    if lead:
        copies[2].wait()
        copies[3].wait()
    for copy in leaving:
        copy.wait()


def step(dims, k_turn, tick, last, info, operands, after, effort, pieces):
    side, pitch, groups, width, shares = dims
    pixels, rows = side * side, side * pitch
    depth = -(-rows // 128) * 128
    first, lead, final = tick == 0, tick == 0 and not after, last and k_turn == 0
    in_vmem = pl.BlockSpec(memory_space=VMEM)
    anywhere = pl.BlockSpec(memory_space=ANY)

    def local(array):
        return pltpu.with_memory_space_constraint(array, VMEM)

    def far(array):
        return pltpu.with_memory_space_constraint(array, HBM)

    sums = (2, 9, width, width)
    specs, args = [pl.BlockSpec(memory_space=pltpu.SMEM)], [info]

    def give(array, where, spec):
        args.append(where(array))
        specs.append(spec)

    if first:
        state, *filters = operands
        give(state, far if lead else local, anywhere if lead else in_vmem)
        for f in filters:
            give(f, far if lead else local, anywhere if lead else in_vmem)
    else:
        moved, arriving, packed, before, *others = operands
        give(moved, lambda x: x, in_vmem)
        give(arriving, local, in_vmem)
        for x in (packed, before, *others):
            give(x, local, in_vmem)
    for x in after:
        give(x, lambda x: x, anywhere)

    if final:
        out_shape, out_specs = [jax.ShapeDtypeStruct((4, pixels * groups, width), F32)], [anywhere]
    else:
        out_shape, out_specs = [VMEM((4 * pixels, width), F32)], [in_vmem]
    if first:
        out_shape.append(VMEM((4, 3, 3 * width, 2 * width), BF16))
        if lead:
            out_shape += [VMEM((2, 9, groups * width, width), F32), VMEM((4, pixels * groups, width), F32)]
    if last:
        part = (2, 9, width // shares, width)
        if pieces == 0:
            out_shape.append(VMEM((shares, *part), F32))
        else:
            out_shape += [VMEM(part, F32)] + [VMEM(part if pieces == 1 else part[1:], F32)] * (pieces * (shares - 1))
    else:
        out_shape.append(VMEM(sums, F32))
    out_specs += [in_vmem] * (len(out_shape) - 1)

    scratch = [VMEM((4, rows, width), F32)] + [VMEM((2 * pitch + depth, 6 * width), BF16)] * 3 + [pltpu.SemaphoreType.DMA((6,)), VMEM((rows + 16, width), F32)]
    if lead:
        scratch.append(VMEM(sums, F32))
    if last:
        scratch.append(VMEM(sums, F32))
    if final:
        scratch.append(VMEM((4, pixels * groups, width), F32))
    return pl.pallas_call(
        functools.partial(step_kernel, dims, k_turn, tick, last, len(after), pieces),
        out_shape=out_shape,
        in_specs=specs,
        out_specs=out_specs,
        scratch_shapes=scratch,
        compiler_params=pltpu.CompilerParams(vmem_limit_bytes=VMEM_LIMIT),
        cost_estimate=pl.CostEstimate(flops=effort, bytes_accessed=1, transcendentals=0),
        name=f"tick_{tick}_turn_{k_turn}",
    )(*args)


def add_kernel(stacked, n_terms, n_parts, n_after, *refs):
    outs = refs[n_terms + n_parts + n_after :]
    for k in range(2):
        terms = [refs[0][n, k] for n in range(refs[0].shape[0])] if stacked else [refs[0][k]]
        terms += [ref[k] for ref in refs[1:n_terms]] + [ref[...] for ref in refs[n_terms + k : n_terms + n_parts : 2]]
        total = functools.reduce(lambda x, y: x + y, terms)
        if len(outs) > 1:
            outs[k][...] = total
        else:
            outs[0][k] = total


def add(stacked, terms, parts, after, effort, out, name):
    in_vmem = pl.BlockSpec(memory_space=VMEM)
    return pl.pallas_call(
        functools.partial(add_kernel, stacked, len(terms), len(parts), len(after)),
        out_shape=out,
        in_specs=[in_vmem] * (len(terms) + len(parts)) + [pl.BlockSpec(memory_space=ANY)] * len(after),
        out_specs=[in_vmem] * len(out) if isinstance(out, list) else in_vmem,
        compiler_params=pltpu.CompilerParams(vmem_limit_bytes=VMEM_LIMIT),
        cost_estimate=pl.CostEstimate(flops=effort, bytes_accessed=1, transcendentals=0),
        name=name,
    )(*terms, *parts, *after)


def on_device(section_state, arriving, first_weight, second_weight):
    _, _, _, pixels, channels = section_state.shape
    width = first_weight.shape[-1]
    groups = channels // width
    side = math.isqrt(pixels)
    pitch = -(-(side + 1) // 16) * 16
    sections, reps = lax.axis_size("section"), lax.axis_size("rep")
    shares = reps // groups
    dims = (side, pitch, groups, width, shares)
    ticks = arriving.shape[0] + 1

    state = section_state[0].reshape(4, pixels * groups, width)
    arrivals = arriving.reshape(ticks - 1, 4, pixels * groups, width)
    filters = (first_weight[0, 0], second_weight[0, 0])

    rep = lax.axis_index("rep")
    at_end = lax.axis_index("section") == sections - 1
    info = jnp.stack([rep // shares, at_end.astype(jnp.int32), rep % shares]).astype(jnp.int32)

    turns = list(range(groups - 1, -1, -1))
    down = [(s, s - 1) for s in range(1, sections)]
    moved, packed, sums, outs, totals, waiting, mine = {}, {}, {}, {}, {}, {}, None

    def swap(part, d):
        return lax.ppermute(part, "rep", [(r, r - r % shares + (r % shares + d) % shares) for r in range(reps)])

    order = PLAN["order"] or sorted(((t, p) for t in range(ticks) for p in range(groups)), key=lambda i: (i[1] + 2 * i[0], -i[0]))
    part = (2, 9, width // shares, width)
    previous = None
    for item in order:
        tick, p = item
        k, last = turns[p], tick == ticks - 1
        after = waiting.pop(item, []) + ([] if previous is None else [previous])
        effort, pieces = PLAN["step"].get(item, 1), PLAN["swap"].get(p, 2)
        if tick == 0:
            results = list(step(dims, k, tick, last, info, (state, *filters), after, effort, pieces))
            if previous is None:
                filters, state = (results.pop(2),), results.pop(2)
            out, packed[p], *grads = results
        else:
            others = [outs[o] for o in range(p)] if last and k == 0 else []
            out, *grads = step(dims, k, tick, last, info, (moved[p], arrivals, packed[p], sums[p], *others), after, effort, pieces)
        previous = out
        if not last:
            sums[p] = grads[0]
            moved[p] = lax.ppermute(out, "section", down)
            continue
        outs[p] = out
        terms, parts = [grads[0]], []
        if pieces == 0:
            chips = [list(range(low, low + shares)) for low in range(0, reps, shares)]
            terms = [lax.all_to_all(grads[0], "rep", 0, 0, axis_index_groups=chips)]
        else:
            parts = [swap(x, 1 + h // pieces) for h, x in enumerate(grads[1:])]
            if pieces == 1:
                terms, parts = terms + parts, []
        if k == 0:
            mine, swapped = terms[0], parts
            break
        if p == 1:
            terms.append(totals.pop(0))
        after = [moved[q] for q in PLAN["wait"].get(p, [])]
        total = add(pieces == 0, terms, parts, after, PLAN["add"].get(p, 1), VMEM(part, F32), f"add_turn_{k}")
        if p in PLAN["need"]:
            waiting.setdefault(PLAN["need"][p], []).append(total)
        mask = 1 if p == 0 else k
        totals[p] = lax.ppermute(total, "rep", [(r, (r // shares ^ mask) * shares + r % shares) for r in range(reps)])
        if p in PLAN["znd"]:
            waiting.setdefault(PLAN["znd"][p], []).append(totals[p])

    kept = add(False, [mine, *totals.values()], [], [], PLAN["sum"], VMEM(part, F32), "add_arrived")
    out = [jax.ShapeDtypeStruct(part[1:], F32)] * 2
    first_grad, second_grad = add(False, [kept], swapped, [], PLAN["last"], out, "add_last")
    returned = outs[groups - 1].reshape(1, 4, 1, pixels, channels)
    return (returned, first_grad[None, None], second_grad[None, None])


def solution(mesh):
    return jax.shard_map(
        on_device,
        mesh=mesh,
        in_specs=(
            P("section", None, "rep", None, None),
            P(None, None, "rep", None, None),
            P("section", None, None, None, None),
            P("section", None, None, None, None),
        ),
        out_specs=(
            P("section", None, "rep", None, None),
            P("section", None, None, "rep", None),
            P("section", None, None, "rep", None),
        ),
        check_vma=False,
    )
```

```python
import functools
import math

import jax
import jax.numpy as jnp
from jax import lax
from jax.experimental import pallas as pl
from jax.experimental.pallas import tpu as pltpu
from jax.sharding import PartitionSpec as P

F32, BF16 = jnp.float32, jnp.bfloat16
VMEM_LIMIT = 8 * 2**20
VMEM, HBM, ANY = pltpu.VMEM, pltpu.HBM, pl.ANY
PLAN = {'step': {(0, 0): 10000000000, (0, 2): 1000000000, (0, 3): 1000000000, (2, 1): 1000000000, (1, 2): 100000000000}, 'add': {1: 100000000000, 2: 1000000000, 3: 1000000000}, 'need': {0: (2, 1), 1: (2, 2), 2: (2, 3)}, 'wait': {}, 'znd': {}, 'swap': {3: 2, 0: 2, 1: 1, 2: 2}, 'sum': 1, 'last': 1, 'order': ((0, 0), (0, 2), (0, 1), (1, 0), (1, 1), (0, 3), (2, 0), (2, 1), (1, 2), (1, 3), (2, 2), (2, 3))}


def halves(value):
    high = value.astype(BF16)
    return high, (value - high.astype(F32)).astype(BF16)


def spread(taps, value, pitch, shifted):
    rows, width = value.shape
    shifted[8 : 8 + rows, :] = value
    for b in range(3):
        moved = value if b == 1 else shifted[7 + b : 7 + b + rows, :]
        for k, half in enumerate(halves(moved)):
            low = (3 * k + b) * width
            taps[pitch : pitch + rows, low : low + width] = half


def conv(taps, packed, rows, pitch):
    total = None
    for a in range(3):
        filters = packed[a]
        part = jnp.dot(
            taps[a * pitch : a * pitch + rows, :], jnp.concatenate([filters, filters], axis=0), preferred_element_type=F32
        )
        total = part if total is None else total + part
    width = total.shape[1] // 2
    return total[:, :width] + total[:, width:]


def turn(value, depth):
    rows, width = value.shape
    high, low = halves(jnp.concatenate([value, jnp.zeros((depth - rows, width), F32)], axis=0).T)
    return jnp.concatenate([high, high, low], axis=1)


def step_kernel(dims, k_turn, tick, last, n_after, pieces, *refs):
    side, pitch, groups, width, shares = dims
    rows, pixels = side * pitch, side * side
    depth = -(-rows // 128) * 128
    first, lead, final = tick == 0, tick == 0 and n_after == 0, last and k_turn == 0
    refs = list(refs)
    take = lambda n: [refs.pop(0) for _ in range(n)]
    (info,) = take(1)
    if first:
        (state,) = take(1)
        filters = take(2 if lead else 1)
    else:
        moved, arriving, packed, sums_in = take(4)
    others = take(groups - 1) if final else []
    take(n_after)
    (out,) = take(1)
    if first:
        (packed,) = take(1)
        if lead:
            kept, kept_state = take(2)
    if last:
        grads = take(1 + pieces * (shares - 1))
    else:
        (sums,) = take(1)
    plane, taps_one, taps_two, taps_error, sems, shifted = take(6)
    shifted[0:8, :] = jnp.zeros((8, width), F32)
    shifted[8 + rows :, :] = jnp.zeros((8, width), F32)
    if lead:
        (weights,) = take(1)
    if last:
        (sums,) = take(1)
    if final:
        (whole,) = take(1)

    group = info[0] ^ k_turn
    channels = pl.ds(pl.multiple_of(group * width, width), width)
    if lead:
        copies = [pltpu.make_async_copy(f.at[:, channels, :], weights.at[k], sems.at[k]) for k, f in enumerate(filters)]
        copies += [pltpu.make_async_copy(f, kept.at[k], sems.at[2 + k]) for k, f in enumerate(filters)]
        from_state = pltpu.make_async_copy(state, kept_state, sems.at[4])
        from_state.start()
        for copy in copies:
            copy.start()
    if not first:
        at_end = info[1] == 1
    for taps in (taps_one, taps_two, taps_error):
        taps[0:pitch, :] = jnp.zeros((pitch, 6 * width), BF16)
        low = pitch + rows
        taps[low:, :] = jnp.zeros((taps.shape[0] - low, 6 * width), BF16)
    for member in range(4):
        for r in range(side):
            plane[member, r * pitch + side : (r + 1) * pitch, :] = jnp.zeros((pitch - side, width), F32)

    if lead:
        from_state.wait()
        state = kept_state
    for member in range(4):
        for r in range(side):
            low = member * pixels + r * side
            strided = pl.ds(r * side * groups + group, side, stride=groups)
            if first:
                row = state[member, strided, :]
            else:
                row = jnp.where(at_end, arriving[tick - 1, member, strided, :], moved[low : low + side, :])
            plane[member, r * pitch : r * pitch + side, :] = row

    inside = lax.rem(lax.broadcasted_iota(jnp.int32, (rows, width), 0), pitch) < side

    def branch(value):
        gate = 1.0 / (1.0 + jnp.exp(-value))
        return value * gate, gate * (1.0 + value * (1.0 - gate))

    leaving = []

    def give(member, value):
        if final:
            for slot, other in enumerate(others):
                theirs = info[0] ^ (groups - 1 - slot)
                whole[member, pl.ds(theirs, pixels, stride=groups), :] = other[member * pixels : (member + 1) * pixels, :]
        for r in range(side):
            piece = value[r * pitch : r * pitch + side, :]
            if final:
                whole[member, pl.ds(r * side * groups + group, side, stride=groups), :] = piece
            else:
                low = member * pixels + r * side
                out[low : low + side, :] = piece
        if final:
            copy = pltpu.make_async_copy(whole.at[member], out.at[member], sems.at[1 + member])
            copy.start()
            leaving.append(copy)

    def pack(k):
        for t in range(9):
            if lead:
                tap, mirror = weights[k, t], weights[k, 8 - t]
            else:
                tap, mirror = filters[0][k, t, channels, :], filters[0][k, 8 - t, channels, :]
            a, b = divmod(t, 3)
            packed[k, a, b * width : (b + 1) * width, :] = jnp.concatenate(halves(tap.T), axis=1)
            packed[2 + k, a, b * width : (b + 1) * width, :] = jnp.concatenate(halves(mirror), axis=1)

    def filter_grads(k, change, taps):
        turned = turn(change, depth)
        for a in range(3):
            high = taps[a * pitch : a * pitch + depth, : 3 * width]
            low = taps[a * pitch : a * pitch + depth, 3 * width :]
            grad = jnp.dot(turned, jnp.concatenate([high, low, high], axis=0), preferred_element_type=F32)
            for b in range(3):
                tap = grad[:, b * width : (b + 1) * width]
                sums[k, 3 * a + b] = tap if first else tap + sums_in[k, 3 * a + b]

    spread(taps_one, plane[0], pitch, shifted)
    if first:
        if lead:
            copies[1].wait()
        pack(1)
    act, slope_two = branch(conv(taps_one, packed.at[1], rows, pitch))
    x_two = jnp.where(inside, plane[1] - act, 0.0)
    spread(taps_two, x_two, pitch, shifted)
    give(1, x_two)
    change_two = jnp.where(inside, plane[3] * slope_two, 0.0)
    spread(taps_error, change_two, pitch, shifted)
    if first:
        if lead:
            copies[0].wait()
        pack(0)
    raw_one = conv(taps_two, packed.at[0], rows, pitch)
    raw_error = conv(taps_error, packed.at[3], rows, pitch)
    act, slope_one = branch(raw_one)
    give(0, plane[0] - act)
    d_one = jnp.where(inside, plane[2] + raw_error, 0.0)
    give(2, d_one)
    filter_grads(1, change_two, taps_one)
    change_one = jnp.where(inside, d_one * slope_one, 0.0)
    spread(taps_error, change_one, pitch, shifted)
    give(3, plane[3] + conv(taps_error, packed.at[2], rows, pitch))

    filter_grads(0, change_one, taps_two)
    if last:
        part = width // shares
        for d in range(shares):
            rows_of = pl.ds(pl.multiple_of(lax.rem(info[2] + d, shares) * part, part), part)
            if pieces == 0:
                grads[0][d] = sums[:, :, d * part : (d + 1) * part, :]
            elif d == 0 or pieces == 1:
                grads[d][...] = sums[:, :, rows_of, :]
            else:
                for k in range(2):
                    grads[2 * d - 1 + k][...] = sums[k, :, rows_of, :]
    if lead:
        copies[2].wait()
        copies[3].wait()
    for copy in leaving:
        copy.wait()


def step(dims, k_turn, tick, last, info, operands, after, effort, pieces):
    side, pitch, groups, width, shares = dims
    pixels, rows = side * side, side * pitch
    depth = -(-rows // 128) * 128
    first, lead, final = tick == 0, tick == 0 and not after, last and k_turn == 0
    in_vmem = pl.BlockSpec(memory_space=VMEM)
    anywhere = pl.BlockSpec(memory_space=ANY)

    def local(array):
        return pltpu.with_memory_space_constraint(array, VMEM)

    def far(array):
        return pltpu.with_memory_space_constraint(array, HBM)

    sums = (2, 9, width, width)
    specs, args = [pl.BlockSpec(memory_space=pltpu.SMEM)], [info]

    def give(array, where, spec):
        args.append(where(array))
        specs.append(spec)

    if first:
        state, *filters = operands
        give(state, far if lead else local, anywhere if lead else in_vmem)
        for f in filters:
            give(f, far if lead else local, anywhere if lead else in_vmem)
    else:
        moved, arriving, packed, before, *others = operands
        give(moved, lambda x: x, in_vmem)
        give(arriving, local, in_vmem)
        for x in (packed, before, *others):
            give(x, local, in_vmem)
    for x in after:
        give(x, lambda x: x, anywhere)

    if final:
        out_shape, out_specs = [jax.ShapeDtypeStruct((4, pixels * groups, width), F32)], [anywhere]
    else:
        out_shape, out_specs = [VMEM((4 * pixels, width), F32)], [in_vmem]
    if first:
        out_shape.append(VMEM((4, 3, 3 * width, 2 * width), BF16))
        if lead:
            out_shape += [VMEM((2, 9, groups * width, width), F32), VMEM((4, pixels * groups, width), F32)]
    if last:
        part = (2, 9, width // shares, width)
        if pieces == 0:
            out_shape.append(VMEM((shares, *part), F32))
        else:
            out_shape += [VMEM(part, F32)] + [VMEM(part if pieces == 1 else part[1:], F32)] * (pieces * (shares - 1))
    else:
        out_shape.append(VMEM(sums, F32))
    out_specs += [in_vmem] * (len(out_shape) - 1)

    scratch = [VMEM((4, rows, width), F32)] + [VMEM((2 * pitch + depth, 6 * width), BF16)] * 3 + [pltpu.SemaphoreType.DMA((6,)), VMEM((rows + 16, width), F32)]
    if lead:
        scratch.append(VMEM(sums, F32))
    if last:
        scratch.append(VMEM(sums, F32))
    if final:
        scratch.append(VMEM((4, pixels * groups, width), F32))
    return pl.pallas_call(
        functools.partial(step_kernel, dims, k_turn, tick, last, len(after), pieces),
        out_shape=out_shape,
        in_specs=specs,
        out_specs=out_specs,
        scratch_shapes=scratch,
        compiler_params=pltpu.CompilerParams(vmem_limit_bytes=VMEM_LIMIT),
        cost_estimate=pl.CostEstimate(flops=effort, bytes_accessed=1, transcendentals=0),
        name=f"tick_{tick}_turn_{k_turn}",
    )(*args)


def add_kernel(stacked, n_terms, n_parts, n_after, *refs):
    outs = refs[n_terms + n_parts + n_after :]
    for k in range(2):
        terms = [refs[0][n, k] for n in range(refs[0].shape[0])] if stacked else [refs[0][k]]
        terms += [ref[k] for ref in refs[1:n_terms]] + [ref[...] for ref in refs[n_terms + k : n_terms + n_parts : 2]]
        total = functools.reduce(lambda x, y: x + y, terms)
        if len(outs) > 1:
            outs[k][...] = total
        else:
            outs[0][k] = total


def arrived_kernel(info, mine, beside, relayed, far, out):
    outer = jnp.logical_or(info[0] == 0, info[0] == 3)
    for k in range(2):
        out[k] = mine[k] + beside[k] + relayed[k] + jnp.where(outer, far[k], 0.0)


def add(stacked, terms, parts, after, effort, out, name):
    in_vmem = pl.BlockSpec(memory_space=VMEM)
    return pl.pallas_call(
        functools.partial(add_kernel, stacked, len(terms), len(parts), len(after)),
        out_shape=out,
        in_specs=[in_vmem] * (len(terms) + len(parts)) + [pl.BlockSpec(memory_space=ANY)] * len(after),
        out_specs=[in_vmem] * len(out) if isinstance(out, list) else in_vmem,
        compiler_params=pltpu.CompilerParams(vmem_limit_bytes=VMEM_LIMIT),
        cost_estimate=pl.CostEstimate(flops=effort, bytes_accessed=1, transcendentals=0),
        name=name,
    )(*terms, *parts, *after)


def on_device(section_state, arriving, first_weight, second_weight):
    _, _, _, pixels, channels = section_state.shape
    width = first_weight.shape[-1]
    groups = channels // width
    side = math.isqrt(pixels)
    pitch = -(-(side + 1) // 16) * 16
    sections, reps = lax.axis_size("section"), lax.axis_size("rep")
    shares = reps // groups
    dims = (side, pitch, groups, width, shares)
    ticks = arriving.shape[0] + 1

    state = section_state[0].reshape(4, pixels * groups, width)
    arrivals = arriving.reshape(ticks - 1, 4, pixels * groups, width)
    filters = (first_weight[0, 0], second_weight[0, 0])

    rep = lax.axis_index("rep")
    at_end = lax.axis_index("section") == sections - 1
    info = jnp.stack([rep // shares, at_end.astype(jnp.int32), rep % shares]).astype(jnp.int32)

    turns = list(range(groups - 1, -1, -1))
    down = [(s, s - 1) for s in range(1, sections)]
    moved, packed, sums, outs, totals, waiting, mine = {}, {}, {}, {}, {}, {}, None

    def swap(part, d):
        return lax.ppermute(part, "rep", [(r, r - r % shares + (r % shares + d) % shares) for r in range(reps)])

    def between(total, keepers):
        return lax.ppermute(total, "rep", [(a * shares + n, b * shares + n) for a, b in keepers for n in range(shares)])

    order = PLAN["order"] or sorted(((t, p) for t in range(ticks) for p in range(groups)), key=lambda i: (i[1] + 2 * i[0], -i[0]))
    part = (2, 9, width // shares, width)
    previous = None
    for item in order:
        tick, p = item
        k, last = turns[p], tick == ticks - 1
        after = waiting.pop(item, []) + ([] if previous is None else [previous])
        effort, pieces = PLAN["step"].get(item, 1), PLAN["swap"].get(p, 2)
        if tick == 0:
            results = list(step(dims, k, tick, last, info, (state, *filters), after, effort, pieces))
            if previous is None:
                filters, state = (results.pop(2),), results.pop(2)
            out, packed[p], *grads = results
        else:
            others = [outs[o] for o in range(p)] if last and k == 0 else []
            out, *grads = step(dims, k, tick, last, info, (moved[p], arrivals, packed[p], sums[p], *others), after, effort, pieces)
        previous = out
        if not last:
            sums[p] = grads[0]
            moved[p] = lax.ppermute(out, "section", down)
            continue
        outs[p] = out
        terms, parts = [grads[0]], []
        if pieces == 0:
            chips = [list(range(low, low + shares)) for low in range(0, reps, shares)]
            terms = [lax.all_to_all(grads[0], "rep", 0, 0, axis_index_groups=chips)]
        else:
            parts = [swap(x, 1 + h // pieces) for h, x in enumerate(grads[1:])]
            if pieces == 1:
                terms, parts = terms + parts, []
        if k == 0:
            mine, swapped = terms[0], parts
            break
        if p == 1:
            terms.append(totals[0])
        after = [moved[q] for q in PLAN["wait"].get(p, [])]
        own_total = add(pieces == 0, terms, parts, after, PLAN["add"].get(p, 1), VMEM(part, F32), f"add_turn_{k}")
        if p in PLAN["need"]:
            waiting.setdefault(PLAN["need"][p], []).append(own_total)
        if p == 0:
            first_total = own_total
            totals[0] = between(own_total, [(0, 1), (3, 2)])
        elif p == 1:
            totals[1] = between(own_total, [(0, 1), (3, 2), (1, 3), (2, 0)])
            relay = add(False, [first_total, totals[1]], [], [], PLAN["add"].get(3, 1), VMEM(part, F32), "add_relay")
            if 3 in PLAN["need"]:
                waiting.setdefault(PLAN["need"][3], []).append(relay)
            totals[3] = between(relay, [(1, 2), (2, 1)])
        else:
            totals[2] = between(own_total, [(0, 1), (1, 0), (2, 3), (3, 2)])

    in_vmem = pl.BlockSpec(memory_space=VMEM)
    kept = pl.pallas_call(
        arrived_kernel,
        out_shape=VMEM(part, F32),
        in_specs=[pl.BlockSpec(memory_space=pltpu.SMEM)] + [in_vmem] * 4,
        out_specs=in_vmem,
        compiler_params=pltpu.CompilerParams(vmem_limit_bytes=VMEM_LIMIT),
        cost_estimate=pl.CostEstimate(flops=PLAN["sum"], bytes_accessed=1, transcendentals=0),
        name="add_arrived",
    )(info, mine, totals[2], totals[3], totals[1])
    out = [jax.ShapeDtypeStruct(part[1:], F32)] * 2
    first_grad, second_grad = add(False, [kept], swapped, [], PLAN["last"], out, "add_last")
    returned = outs[groups - 1].reshape(1, 4, 1, pixels, channels)
    return (returned, first_grad[None, None], second_grad[None, None])


def solution(mesh):
    return jax.shard_map(
        on_device,
        mesh=mesh,
        in_specs=(
            P("section", None, "rep", None, None),
            P(None, None, "rep", None, None),
            P("section", None, None, None, None),
            P("section", None, None, None, None),
        ),
        out_specs=(
            P("section", None, "rep", None, None),
            P("section", None, None, "rep", None),
            P("section", None, None, "rep", None),
        ),
        check_vma=False,
    )
```

```python
import functools
import math

import jax
import jax.numpy as jnp
from jax import lax
from jax.experimental import pallas as pl
from jax.experimental.pallas import tpu as pltpu
from jax.sharding import PartitionSpec as P

F32, BF16 = jnp.float32, jnp.bfloat16
VMEM_LIMIT = 8 * 2**20
VMEM, HBM, ANY = pltpu.VMEM, pltpu.HBM, pl.ANY
PLAN = {'step': {(0, 0): 10000000000, (0, 2): 1000000000, (0, 3): 1000000000, (2, 1): 1000000000, (1, 2): 100000000000}, 'add': {1: 100000000000, 2: 1000000000, 3: 1000000000}, 'need': {0: (2, 1), 1: (2, 2), 2: (2, 3)}, 'wait': {}, 'znd': {}, 'swap': {3: 2, 0: 2, 1: 1, 2: 2}, 'sum': 1, 'last': 1, 'order': ((0, 0), (0, 2), (0, 1), (1, 0), (1, 1), (0, 3), (2, 0), (2, 1), (1, 2), (1, 3), (2, 2), (2, 3))}


def halves(value):
    high = value.astype(BF16)
    return high, (value - high.astype(F32)).astype(BF16)


def spread(taps, value, pitch, shifted):
    rows, width = value.shape
    shifted[8 : 8 + rows, :] = value
    for b in range(3):
        moved = value if b == 1 else shifted[7 + b : 7 + b + rows, :]
        for k, half in enumerate(halves(moved)):
            low = (3 * k + b) * width
            taps[pitch : pitch + rows, low : low + width] = half


def conv(taps, packed, rows, pitch):
    total = None
    for a in range(3):
        filters = packed[a]
        part = jnp.dot(
            taps[a * pitch : a * pitch + rows, :], jnp.concatenate([filters, filters], axis=0), preferred_element_type=F32
        )
        total = part if total is None else total + part
    width = total.shape[1] // 2
    return total[:, :width] + total[:, width:]


def turn(value, depth):
    rows, width = value.shape
    high, low = halves(jnp.concatenate([value, jnp.zeros((depth - rows, width), F32)], axis=0).T)
    return jnp.concatenate([high, high, low], axis=1)


def step_kernel(dims, k_turn, tick, last, n_after, pieces, *refs):
    side, pitch, groups, width, shares = dims
    rows, pixels = side * pitch, side * side
    depth = -(-rows // 128) * 128
    first, lead, final = tick == 0, tick == 0 and n_after == 0, last and k_turn == 0
    refs = list(refs)
    take = lambda n: [refs.pop(0) for _ in range(n)]
    (info,) = take(1)
    if first:
        (state,) = take(1)
        filters = take(2 if lead else 1)
    else:
        moved, arriving, packed, sums_in = take(4)
    others = take(groups - 1) if final else []
    take(n_after)
    (out,) = take(1)
    if first:
        (packed,) = take(1)
        if lead:
            kept, kept_state = take(2)
    if last:
        grads = take(1 + pieces * (shares - 1))
    else:
        (sums,) = take(1)
    plane, taps_one, taps_two, taps_error, sems, shifted = take(6)
    shifted[0:8, :] = jnp.zeros((8, width), F32)
    shifted[8 + rows :, :] = jnp.zeros((8, width), F32)
    if lead:
        (weights,) = take(1)
    if last:
        (sums,) = take(1)
    if final:
        (whole,) = take(1)

    group = info[0] ^ k_turn
    channels = pl.ds(pl.multiple_of(group * width, width), width)
    if lead:
        copies = [pltpu.make_async_copy(f.at[:, channels, :], weights.at[k], sems.at[k]) for k, f in enumerate(filters)]
        copies += [pltpu.make_async_copy(f, kept.at[k], sems.at[2 + k]) for k, f in enumerate(filters)]
        from_state = pltpu.make_async_copy(state, kept_state, sems.at[4])
        from_state.start()
        copies[1].start()
        copies[0].start()
    if not first:
        at_end = info[1] == 1
    for taps in (taps_one, taps_two, taps_error):
        taps[0:pitch, :] = jnp.zeros((pitch, 6 * width), BF16)
        low = pitch + rows
        taps[low:, :] = jnp.zeros((taps.shape[0] - low, 6 * width), BF16)
    for member in range(4):
        for r in range(side):
            plane[member, r * pitch + side : (r + 1) * pitch, :] = jnp.zeros((pitch - side, width), F32)

    if lead:
        from_state.wait()
        state = kept_state
    for member in range(4):
        for r in range(side):
            low = member * pixels + r * side
            strided = pl.ds(r * side * groups + group, side, stride=groups)
            if first:
                row = state[member, strided, :]
            else:
                row = jnp.where(at_end, arriving[tick - 1, member, strided, :], moved[low : low + side, :])
            plane[member, r * pitch : r * pitch + side, :] = row

    inside = lax.rem(lax.broadcasted_iota(jnp.int32, (rows, width), 0), pitch) < side

    def branch(value):
        gate = 1.0 / (1.0 + jnp.exp(-value))
        return value * gate, gate * (1.0 + value * (1.0 - gate))

    leaving = []

    def give(member, value):
        if final:
            for slot, other in enumerate(others):
                theirs = info[0] ^ (groups - 1 - slot)
                whole[member, pl.ds(theirs, pixels, stride=groups), :] = other[member * pixels : (member + 1) * pixels, :]
        for r in range(side):
            piece = value[r * pitch : r * pitch + side, :]
            if final:
                whole[member, pl.ds(r * side * groups + group, side, stride=groups), :] = piece
            else:
                low = member * pixels + r * side
                out[low : low + side, :] = piece
        if final:
            copy = pltpu.make_async_copy(whole.at[member], out.at[member], sems.at[1 + member])
            copy.start()
            leaving.append(copy)

    def pack(k):
        for t in range(9):
            if lead:
                tap, mirror = weights[k, t], weights[k, 8 - t]
            else:
                tap, mirror = filters[0][k, t, channels, :], filters[0][k, 8 - t, channels, :]
            a, b = divmod(t, 3)
            packed[k, a, b * width : (b + 1) * width, :] = jnp.concatenate(halves(tap.T), axis=1)
            packed[2 + k, a, b * width : (b + 1) * width, :] = jnp.concatenate(halves(mirror), axis=1)

    def filter_grads(k, change, taps):
        turned = turn(change, depth)
        for a in range(3):
            high = taps[a * pitch : a * pitch + depth, : 3 * width]
            low = taps[a * pitch : a * pitch + depth, 3 * width :]
            grad = jnp.dot(turned, jnp.concatenate([high, low, high], axis=0), preferred_element_type=F32)
            for b in range(3):
                tap = grad[:, b * width : (b + 1) * width]
                sums[k, 3 * a + b] = tap if first else tap + sums_in[k, 3 * a + b]

    spread(taps_one, plane[0], pitch, shifted)
    if first:
        if lead:
            copies[1].wait()
            copies[0].wait()
            copies[2].start()
            copies[3].start()
        pack(1)
    act, slope_two = branch(conv(taps_one, packed.at[1], rows, pitch))
    x_two = jnp.where(inside, plane[1] - act, 0.0)
    spread(taps_two, x_two, pitch, shifted)
    give(1, x_two)
    change_two = jnp.where(inside, plane[3] * slope_two, 0.0)
    spread(taps_error, change_two, pitch, shifted)
    if first:
        pack(0)
    raw_one = conv(taps_two, packed.at[0], rows, pitch)
    raw_error = conv(taps_error, packed.at[3], rows, pitch)
    act, slope_one = branch(raw_one)
    give(0, plane[0] - act)
    d_one = jnp.where(inside, plane[2] + raw_error, 0.0)
    give(2, d_one)
    filter_grads(1, change_two, taps_one)
    change_one = jnp.where(inside, d_one * slope_one, 0.0)
    spread(taps_error, change_one, pitch, shifted)
    give(3, plane[3] + conv(taps_error, packed.at[2], rows, pitch))

    filter_grads(0, change_one, taps_two)
    if last:
        part = width // shares
        for d in range(shares):
            rows_of = pl.ds(pl.multiple_of(lax.rem(info[2] + d, shares) * part, part), part)
            if pieces == 0:
                grads[0][d] = sums[:, :, d * part : (d + 1) * part, :]
            elif d == 0 or pieces == 1:
                grads[d][...] = sums[:, :, rows_of, :]
            else:
                for k in range(2):
                    grads[2 * d - 1 + k][...] = sums[k, :, rows_of, :]
    if lead:
        copies[2].wait()
        copies[3].wait()
    for copy in leaving:
        copy.wait()


def step(dims, k_turn, tick, last, info, operands, after, effort, pieces):
    side, pitch, groups, width, shares = dims
    pixels, rows = side * side, side * pitch
    depth = -(-rows // 128) * 128
    first, lead, final = tick == 0, tick == 0 and not after, last and k_turn == 0
    in_vmem = pl.BlockSpec(memory_space=VMEM)
    anywhere = pl.BlockSpec(memory_space=ANY)

    def local(array):
        return pltpu.with_memory_space_constraint(array, VMEM)

    def far(array):
        return pltpu.with_memory_space_constraint(array, HBM)

    sums = (2, 9, width, width)
    specs, args = [pl.BlockSpec(memory_space=pltpu.SMEM)], [info]

    def give(array, where, spec):
        args.append(where(array))
        specs.append(spec)

    if first:
        state, *filters = operands
        give(state, far if lead else local, anywhere if lead else in_vmem)
        for f in filters:
            give(f, far if lead else local, anywhere if lead else in_vmem)
    else:
        moved, arriving, packed, before, *others = operands
        give(moved, lambda x: x, in_vmem)
        give(arriving, local, in_vmem)
        for x in (packed, before, *others):
            give(x, local, in_vmem)
    for x in after:
        give(x, lambda x: x, anywhere)

    if final:
        out_shape, out_specs = [jax.ShapeDtypeStruct((4, pixels * groups, width), F32)], [anywhere]
    else:
        out_shape, out_specs = [VMEM((4 * pixels, width), F32)], [in_vmem]
    if first:
        out_shape.append(VMEM((4, 3, 3 * width, 2 * width), BF16))
        if lead:
            out_shape += [VMEM((2, 9, groups * width, width), F32), VMEM((4, pixels * groups, width), F32)]
    if last:
        part = (2, 9, width // shares, width)
        if pieces == 0:
            out_shape.append(VMEM((shares, *part), F32))
        else:
            out_shape += [VMEM(part, F32)] + [VMEM(part if pieces == 1 else part[1:], F32)] * (pieces * (shares - 1))
    else:
        out_shape.append(VMEM(sums, F32))
    out_specs += [in_vmem] * (len(out_shape) - 1)

    scratch = [VMEM((4, rows, width), F32)] + [VMEM((2 * pitch + depth, 6 * width), BF16)] * 3 + [pltpu.SemaphoreType.DMA((6,)), VMEM((rows + 16, width), F32)]
    if lead:
        scratch.append(VMEM(sums, F32))
    if last:
        scratch.append(VMEM(sums, F32))
    if final:
        scratch.append(VMEM((4, pixels * groups, width), F32))
    return pl.pallas_call(
        functools.partial(step_kernel, dims, k_turn, tick, last, len(after), pieces),
        out_shape=out_shape,
        in_specs=specs,
        out_specs=out_specs,
        scratch_shapes=scratch,
        compiler_params=pltpu.CompilerParams(vmem_limit_bytes=VMEM_LIMIT),
        cost_estimate=pl.CostEstimate(flops=effort, bytes_accessed=1, transcendentals=0),
        name=f"tick_{tick}_turn_{k_turn}",
    )(*args)


def add_kernel(stacked, n_terms, n_parts, n_after, *refs):
    outs = refs[n_terms + n_parts + n_after :]
    for k in range(2):
        terms = [refs[0][n, k] for n in range(refs[0].shape[0])] if stacked else [refs[0][k]]
        terms += [ref[k] for ref in refs[1:n_terms]] + [ref[...] for ref in refs[n_terms + k : n_terms + n_parts : 2]]
        total = functools.reduce(lambda x, y: x + y, terms)
        if len(outs) > 1:
            outs[k][...] = total
        else:
            outs[0][k] = total


def last_kernel(info, mine, beside, relayed, far, *refs):
    outer = jnp.logical_or(info[0] == 0, info[0] == 3)
    for k, out in enumerate(refs[-2:]):
        total = mine[k] + beside[k] + relayed[k] + jnp.where(outer, far[k], 0.0)
        out[...] = functools.reduce(lambda x, y: x + y, [ref[...] for ref in refs[k:-2:2]], total)


def add(stacked, terms, parts, after, effort, out, name):
    in_vmem = pl.BlockSpec(memory_space=VMEM)
    return pl.pallas_call(
        functools.partial(add_kernel, stacked, len(terms), len(parts), len(after)),
        out_shape=out,
        in_specs=[in_vmem] * (len(terms) + len(parts)) + [pl.BlockSpec(memory_space=ANY)] * len(after),
        out_specs=[in_vmem] * len(out) if isinstance(out, list) else in_vmem,
        compiler_params=pltpu.CompilerParams(vmem_limit_bytes=VMEM_LIMIT),
        cost_estimate=pl.CostEstimate(flops=effort, bytes_accessed=1, transcendentals=0),
        name=name,
    )(*terms, *parts, *after)


def on_device(section_state, arriving, first_weight, second_weight):
    _, _, _, pixels, channels = section_state.shape
    width = first_weight.shape[-1]
    groups = channels // width
    side = math.isqrt(pixels)
    pitch = -(-(side + 1) // 16) * 16
    sections, reps = lax.axis_size("section"), lax.axis_size("rep")
    shares = reps // groups
    dims = (side, pitch, groups, width, shares)
    ticks = arriving.shape[0] + 1

    state = section_state[0].reshape(4, pixels * groups, width)
    arrivals = arriving.reshape(ticks - 1, 4, pixels * groups, width)
    filters = (first_weight[0, 0], second_weight[0, 0])

    rep = lax.axis_index("rep")
    at_end = lax.axis_index("section") == sections - 1
    info = jnp.stack([rep // shares, at_end.astype(jnp.int32), rep % shares]).astype(jnp.int32)

    turns = list(range(groups - 1, -1, -1))
    down = [(s, s - 1) for s in range(1, sections)]
    moved, packed, sums, outs, totals, waiting, mine = {}, {}, {}, {}, {}, {}, None

    def swap(part, d):
        return lax.ppermute(part, "rep", [(r, r - r % shares + (r % shares + d) % shares) for r in range(reps)])

    def between(total, keepers):
        return lax.ppermute(total, "rep", [(a * shares + n, b * shares + n) for a, b in keepers for n in range(shares)])

    order = PLAN["order"] or sorted(((t, p) for t in range(ticks) for p in range(groups)), key=lambda i: (i[1] + 2 * i[0], -i[0]))
    part = (2, 9, width // shares, width)
    previous = None
    for item in order:
        tick, p = item
        k, last = turns[p], tick == ticks - 1
        after = waiting.pop(item, []) + ([] if previous is None else [previous])
        effort, pieces = PLAN["step"].get(item, 1), PLAN["swap"].get(p, 2)
        if tick == 0:
            results = list(step(dims, k, tick, last, info, (state, *filters), after, effort, pieces))
            if previous is None:
                filters, state = (results.pop(2),), results.pop(2)
            out, packed[p], *grads = results
        else:
            others = [outs[o] for o in range(p)] if last and k == 0 else []
            out, *grads = step(dims, k, tick, last, info, (moved[p], arrivals, packed[p], sums[p], *others), after, effort, pieces)
        previous = out
        if not last:
            sums[p] = grads[0]
            moved[p] = lax.ppermute(out, "section", down)
            continue
        outs[p] = out
        terms, parts = [grads[0]], []
        if pieces == 0:
            chips = [list(range(low, low + shares)) for low in range(0, reps, shares)]
            terms = [lax.all_to_all(grads[0], "rep", 0, 0, axis_index_groups=chips)]
        else:
            parts = [swap(x, 1 + h // pieces) for h, x in enumerate(grads[1:])]
            if pieces == 1:
                terms, parts = terms + parts, []
        if k == 0:
            mine, swapped = terms[0], parts
            break
        if p == 1:
            terms.append(totals[0])
        after = [moved[q] for q in PLAN["wait"].get(p, [])]
        own_total = add(pieces == 0, terms, parts, after, PLAN["add"].get(p, 1), VMEM(part, F32), f"add_turn_{k}")
        if p in PLAN["need"]:
            waiting.setdefault(PLAN["need"][p], []).append(own_total)
        if p == 0:
            first_total = own_total
            totals[0] = between(own_total, [(0, 1), (3, 2)])
        elif p == 1:
            totals[1] = between(own_total, [(0, 1), (3, 2), (1, 3), (2, 0)])
            relay = add(False, [first_total, totals[1]], [], [], PLAN["add"].get(3, 1), VMEM(part, F32), "add_relay")
            if 3 in PLAN["need"]:
                waiting.setdefault(PLAN["need"][3], []).append(relay)
            totals[3] = between(relay, [(1, 2), (2, 1)])
        else:
            totals[2] = between(own_total, [(0, 1), (1, 0), (2, 3), (3, 2)])

    in_vmem = pl.BlockSpec(memory_space=VMEM)
    terms = [mine, totals[2], totals[3], totals[1], *swapped]
    first_grad, second_grad = pl.pallas_call(
        last_kernel,
        out_shape=[jax.ShapeDtypeStruct(part[1:], F32)] * 2,
        in_specs=[pl.BlockSpec(memory_space=pltpu.SMEM)] + [in_vmem] * len(terms),
        out_specs=[in_vmem] * 2,
        compiler_params=pltpu.CompilerParams(vmem_limit_bytes=VMEM_LIMIT),
        cost_estimate=pl.CostEstimate(flops=PLAN["last"], bytes_accessed=1, transcendentals=0),
        name="add_last",
    )(info, *terms)
    returned = outs[groups - 1].reshape(1, 4, 1, pixels, channels)
    return (returned, first_grad[None, None], second_grad[None, None])


def solution(mesh):
    return jax.shard_map(
        on_device,
        mesh=mesh,
        in_specs=(
            P("section", None, "rep", None, None),
            P(None, None, "rep", None, None),
            P("section", None, None, None, None),
            P("section", None, None, None, None),
        ),
        out_specs=(
            P("section", None, "rep", None, None),
            P("section", None, None, "rep", None),
            P("section", None, None, "rep", None),
        ),
        check_vma=False,
    )
```

```python
import functools
import math

import jax
import jax.numpy as jnp
from jax import lax
from jax.experimental import pallas as pl
from jax.experimental.pallas import tpu as pltpu
from jax.sharding import PartitionSpec as P

F32, BF16 = jnp.float32, jnp.bfloat16
VMEM_LIMIT = 8 * 2**20
VMEM, HBM, ANY = pltpu.VMEM, pltpu.HBM, pl.ANY
PLAN = {'step': {(0, 0): 10000000000, (0, 2): 1000000000, (0, 3): 1000000000, (2, 1): 1000000000, (1, 2): 100000000000}, 'add': {1: 100000000000, 2: 1000000000, 3: 1000000000}, 'need': {0: (2, 1), 1: (2, 2), 2: (2, 3)}, 'wait': {}, 'znd': {}, 'swap': {3: 2, 0: 2, 1: 1, 2: 2}, 'sum': 1, 'last': 1, 'order': ((0, 0), (0, 2), (0, 1), (1, 0), (1, 1), (0, 3), (2, 0), (2, 1), (1, 2), (1, 3), (2, 2), (2, 3))}


def halves(value):
    high = value.astype(BF16)
    return high, (value - high.astype(F32)).astype(BF16)


def spread(taps, value, pitch, shifted):
    rows, width = value.shape
    shifted[8 : 8 + rows, :] = value
    for b in range(3):
        moved = value if b == 1 else shifted[7 + b : 7 + b + rows, :]
        for k, half in enumerate(halves(moved)):
            low = (3 * k + b) * width
            taps[pitch : pitch + rows, low : low + width] = half


def conv(taps, packed, rows, pitch):
    total = None
    for a in range(3):
        filters = packed[a]
        part = jnp.dot(
            taps[a * pitch : a * pitch + rows, :], jnp.concatenate([filters, filters], axis=0), preferred_element_type=F32
        )
        total = part if total is None else total + part
    width = total.shape[1] // 2
    return total[:, :width] + total[:, width:]


def turn(value, depth):
    rows, width = value.shape
    high, low = halves(jnp.concatenate([value, jnp.zeros((depth - rows, width), F32)], axis=0).T)
    return jnp.concatenate([high, high, low], axis=1)


def step_kernel(dims, k_turn, tick, last, n_after, pieces, *refs):
    side, pitch, groups, width, shares = dims
    rows, pixels = side * pitch, side * side
    depth = -(-rows // 128) * 128
    first, lead, final = tick == 0, tick == 0 and n_after == 0, last and k_turn == 0
    refs = list(refs)
    take = lambda n: [refs.pop(0) for _ in range(n)]
    (info,) = take(1)
    if first:
        (state,) = take(1)
        filters = take(2 if lead else 1)
    else:
        moved, arriving, packed, sums_in = take(4)
    others = take(groups - 1) if final else []
    take(n_after)
    (out,) = take(1)
    if first:
        (packed,) = take(1)
        if lead:
            kept, kept_state = take(2)
    if last:
        grads = take(1 + pieces * (shares - 1))
    else:
        (sums,) = take(1)
    plane, taps_one, taps_two, taps_error, sems, shifted = take(6)
    shifted[0:8, :] = jnp.zeros((8, width), F32)
    shifted[8 + rows :, :] = jnp.zeros((8, width), F32)
    if lead:
        (weights,) = take(1)
    if last:
        (sums,) = take(1)
    if final:
        (whole,) = take(1)

    group = info[0] ^ k_turn
    channels = pl.ds(pl.multiple_of(group * width, width), width)
    if lead:
        copies = [pltpu.make_async_copy(f.at[:, channels, :], weights.at[k], sems.at[k]) for k, f in enumerate(filters)]
        copies += [pltpu.make_async_copy(f, kept.at[k], sems.at[2 + k]) for k, f in enumerate(filters)]
        from_state = pltpu.make_async_copy(state, kept_state, sems.at[4])
        from_state.start()
        copies[1].start()
        copies[0].start()
    if not first:
        at_end = info[1] == 1
    for taps in (taps_one, taps_two, taps_error):
        taps[0:pitch, :] = jnp.zeros((pitch, 6 * width), BF16)
        low = pitch + rows
        taps[low:, :] = jnp.zeros((taps.shape[0] - low, 6 * width), BF16)
    for member in range(4):
        for r in range(side):
            plane[member, r * pitch + side : (r + 1) * pitch, :] = jnp.zeros((pitch - side, width), F32)

    if lead:
        from_state.wait()
        state = kept_state
    for member in range(4):
        for r in range(side):
            low = member * pixels + r * side
            strided = pl.ds(r * side * groups + group, side, stride=groups)
            if first:
                row = state[member, strided, :]
            else:
                row = jnp.where(at_end, arriving[tick - 1, member, strided, :], moved[low : low + side, :])
            plane[member, r * pitch : r * pitch + side, :] = row

    inside = lax.rem(lax.broadcasted_iota(jnp.int32, (rows, width), 0), pitch) < side

    def branch(value):
        gate = 1.0 / (1.0 + jnp.exp(-value))
        return value * gate, gate * (1.0 + value * (1.0 - gate))

    leaving = []

    def give(member, value):
        if final:
            for slot, other in enumerate(others):
                theirs = info[0] ^ (groups - 1 - slot)
                whole[member, pl.ds(theirs, pixels, stride=groups), :] = other[member * pixels : (member + 1) * pixels, :]
        for r in range(side):
            piece = value[r * pitch : r * pitch + side, :]
            if final:
                whole[member, pl.ds(r * side * groups + group, side, stride=groups), :] = piece
            else:
                low = member * pixels + r * side
                out[low : low + side, :] = piece
        if final:
            copy = pltpu.make_async_copy(whole.at[member], out.at[member], sems.at[1 + member])
            copy.start()
            leaving.append(copy)

    def pack(k):
        for t in range(9):
            if lead:
                tap, mirror = weights[k, t], weights[k, 8 - t]
            else:
                tap, mirror = filters[0][k, t, channels, :], filters[0][k, 8 - t, channels, :]
            a, b = divmod(t, 3)
            packed[k, a, b * width : (b + 1) * width, :] = jnp.concatenate(halves(tap.T), axis=1)
            packed[2 + k, a, b * width : (b + 1) * width, :] = jnp.concatenate(halves(mirror), axis=1)

    def filter_grads(k, change, taps):
        turned = turn(change, depth)
        high, low = (
            jnp.concatenate([taps[a * pitch : a * pitch + depth, 3 * width * h : 3 * width * (h + 1)] for a in range(3)], axis=1)
            for h in range(2)
        )
        grad = jnp.dot(turned, jnp.concatenate([high, low, high], axis=0), preferred_element_type=F32)
        for t in range(9):
            tap = grad[:, t * width : (t + 1) * width]
            sums[k, t] = tap if first else tap + sums_in[k, t]

    spread(taps_one, plane[0], pitch, shifted)
    if first:
        if lead:
            copies[1].wait()
            copies[0].wait()
            copies[2].start()
            copies[3].start()
        pack(1)
    act, slope_two = branch(conv(taps_one, packed.at[1], rows, pitch))
    x_two = jnp.where(inside, plane[1] - act, 0.0)
    spread(taps_two, x_two, pitch, shifted)
    give(1, x_two)
    change_two = jnp.where(inside, plane[3] * slope_two, 0.0)
    spread(taps_error, change_two, pitch, shifted)
    if first:
        pack(0)
    raw_one = conv(taps_two, packed.at[0], rows, pitch)
    raw_error = conv(taps_error, packed.at[3], rows, pitch)
    act, slope_one = branch(raw_one)
    give(0, plane[0] - act)
    d_one = jnp.where(inside, plane[2] + raw_error, 0.0)
    give(2, d_one)
    filter_grads(1, change_two, taps_one)
    change_one = jnp.where(inside, d_one * slope_one, 0.0)
    spread(taps_error, change_one, pitch, shifted)
    give(3, plane[3] + conv(taps_error, packed.at[2], rows, pitch))

    filter_grads(0, change_one, taps_two)
    if last:
        part = width // shares
        for d in range(shares):
            rows_of = pl.ds(pl.multiple_of(lax.rem(info[2] + d, shares) * part, part), part)
            if pieces == 0:
                grads[0][d] = sums[:, :, d * part : (d + 1) * part, :]
            elif d == 0 or pieces == 1:
                grads[d][...] = sums[:, :, rows_of, :]
            else:
                for k in range(2):
                    grads[2 * d - 1 + k][...] = sums[k, :, rows_of, :]
    if lead:
        copies[2].wait()
        copies[3].wait()
    for copy in leaving:
        copy.wait()


def step(dims, k_turn, tick, last, info, operands, after, effort, pieces):
    side, pitch, groups, width, shares = dims
    pixels, rows = side * side, side * pitch
    depth = -(-rows // 128) * 128
    first, lead, final = tick == 0, tick == 0 and not after, last and k_turn == 0
    in_vmem = pl.BlockSpec(memory_space=VMEM)
    anywhere = pl.BlockSpec(memory_space=ANY)

    def local(array):
        return pltpu.with_memory_space_constraint(array, VMEM)

    def far(array):
        return pltpu.with_memory_space_constraint(array, HBM)

    sums = (2, 9, width, width)
    specs, args = [pl.BlockSpec(memory_space=pltpu.SMEM)], [info]

    def give(array, where, spec):
        args.append(where(array))
        specs.append(spec)

    if first:
        state, *filters = operands
        give(state, far if lead else local, anywhere if lead else in_vmem)
        for f in filters:
            give(f, far if lead else local, anywhere if lead else in_vmem)
    else:
        moved, arriving, packed, before, *others = operands
        give(moved, lambda x: x, in_vmem)
        give(arriving, local, in_vmem)
        for x in (packed, before, *others):
            give(x, local, in_vmem)
    for x in after:
        give(x, lambda x: x, anywhere)

    if final:
        out_shape, out_specs = [jax.ShapeDtypeStruct((4, pixels * groups, width), F32)], [anywhere]
    else:
        out_shape, out_specs = [VMEM((4 * pixels, width), F32)], [in_vmem]
    if first:
        out_shape.append(VMEM((4, 3, 3 * width, 2 * width), BF16))
        if lead:
            out_shape += [VMEM((2, 9, groups * width, width), F32), VMEM((4, pixels * groups, width), F32)]
    if last:
        part = (2, 9, width // shares, width)
        if pieces == 0:
            out_shape.append(VMEM((shares, *part), F32))
        else:
            out_shape += [VMEM(part, F32)] + [VMEM(part if pieces == 1 else part[1:], F32)] * (pieces * (shares - 1))
    else:
        out_shape.append(VMEM(sums, F32))
    out_specs += [in_vmem] * (len(out_shape) - 1)

    scratch = [VMEM((4, rows, width), F32)] + [VMEM((2 * pitch + depth, 6 * width), BF16)] * 3 + [pltpu.SemaphoreType.DMA((6,)), VMEM((rows + 16, width), F32)]
    if lead:
        scratch.append(VMEM(sums, F32))
    if last:
        scratch.append(VMEM(sums, F32))
    if final:
        scratch.append(VMEM((4, pixels * groups, width), F32))
    return pl.pallas_call(
        functools.partial(step_kernel, dims, k_turn, tick, last, len(after), pieces),
        out_shape=out_shape,
        in_specs=specs,
        out_specs=out_specs,
        scratch_shapes=scratch,
        compiler_params=pltpu.CompilerParams(vmem_limit_bytes=VMEM_LIMIT),
        cost_estimate=pl.CostEstimate(flops=effort, bytes_accessed=1, transcendentals=0),
        name=f"tick_{tick}_turn_{k_turn}",
    )(*args)


def add_kernel(stacked, n_terms, n_parts, n_after, *refs):
    outs = refs[n_terms + n_parts + n_after :]
    for k in range(2):
        terms = [refs[0][n, k] for n in range(refs[0].shape[0])] if stacked else [refs[0][k]]
        terms += [ref[k] for ref in refs[1:n_terms]] + [ref[...] for ref in refs[n_terms + k : n_terms + n_parts : 2]]
        total = functools.reduce(lambda x, y: x + y, terms)
        if len(outs) > 1:
            outs[k][...] = total
        else:
            outs[0][k] = total


def last_kernel(info, mine, beside, relayed, far, *refs):
    outer = jnp.logical_or(info[0] == 0, info[0] == 3)
    for k, out in enumerate(refs[-2:]):
        total = mine[k] + beside[k] + relayed[k] + jnp.where(outer, far[k], 0.0)
        out[...] = functools.reduce(lambda x, y: x + y, [ref[...] for ref in refs[k:-2:2]], total)


def add(stacked, terms, parts, after, effort, out, name):
    in_vmem = pl.BlockSpec(memory_space=VMEM)
    return pl.pallas_call(
        functools.partial(add_kernel, stacked, len(terms), len(parts), len(after)),
        out_shape=out,
        in_specs=[in_vmem] * (len(terms) + len(parts)) + [pl.BlockSpec(memory_space=ANY)] * len(after),
        out_specs=[in_vmem] * len(out) if isinstance(out, list) else in_vmem,
        compiler_params=pltpu.CompilerParams(vmem_limit_bytes=VMEM_LIMIT),
        cost_estimate=pl.CostEstimate(flops=effort, bytes_accessed=1, transcendentals=0),
        name=name,
    )(*terms, *parts, *after)


def on_device(section_state, arriving, first_weight, second_weight):
    _, _, _, pixels, channels = section_state.shape
    width = first_weight.shape[-1]
    groups = channels // width
    side = math.isqrt(pixels)
    pitch = -(-(side + 1) // 16) * 16
    sections, reps = lax.axis_size("section"), lax.axis_size("rep")
    shares = reps // groups
    dims = (side, pitch, groups, width, shares)
    ticks = arriving.shape[0] + 1

    state = section_state[0].reshape(4, pixels * groups, width)
    arrivals = arriving.reshape(ticks - 1, 4, pixels * groups, width)
    filters = (first_weight[0, 0], second_weight[0, 0])

    rep = lax.axis_index("rep")
    at_end = lax.axis_index("section") == sections - 1
    info = jnp.stack([rep // shares, at_end.astype(jnp.int32), rep % shares]).astype(jnp.int32)

    turns = list(range(groups - 1, -1, -1))
    down = [(s, s - 1) for s in range(1, sections)]
    moved, packed, sums, outs, totals, waiting, mine = {}, {}, {}, {}, {}, {}, None

    def swap(part, d):
        return lax.ppermute(part, "rep", [(r, r - r % shares + (r % shares + d) % shares) for r in range(reps)])

    def between(total, keepers):
        return lax.ppermute(total, "rep", [(a * shares + n, b * shares + n) for a, b in keepers for n in range(shares)])

    order = PLAN["order"] or sorted(((t, p) for t in range(ticks) for p in range(groups)), key=lambda i: (i[1] + 2 * i[0], -i[0]))
    part = (2, 9, width // shares, width)
    previous = None
    for item in order:
        tick, p = item
        k, last = turns[p], tick == ticks - 1
        after = waiting.pop(item, []) + ([] if previous is None else [previous])
        effort, pieces = PLAN["step"].get(item, 1), PLAN["swap"].get(p, 2)
        if tick == 0:
            results = list(step(dims, k, tick, last, info, (state, *filters), after, effort, pieces))
            if previous is None:
                filters, state = (results.pop(2),), results.pop(2)
            out, packed[p], *grads = results
        else:
            others = [outs[o] for o in range(p)] if last and k == 0 else []
            out, *grads = step(dims, k, tick, last, info, (moved[p], arrivals, packed[p], sums[p], *others), after, effort, pieces)
        previous = out
        if not last:
            sums[p] = grads[0]
            moved[p] = lax.ppermute(out, "section", down)
            continue
        outs[p] = out
        terms, parts = [grads[0]], []
        if pieces == 0:
            chips = [list(range(low, low + shares)) for low in range(0, reps, shares)]
            terms = [lax.all_to_all(grads[0], "rep", 0, 0, axis_index_groups=chips)]
        else:
            parts = [swap(x, 1 + h // pieces) for h, x in enumerate(grads[1:])]
            if pieces == 1:
                terms, parts = terms + parts, []
        if k == 0:
            mine, swapped = terms[0], parts
            break
        if p == 1:
            terms.append(totals[0])
        after = [moved[q] for q in PLAN["wait"].get(p, [])]
        own_total = add(pieces == 0, terms, parts, after, PLAN["add"].get(p, 1), VMEM(part, F32), f"add_turn_{k}")
        if p in PLAN["need"]:
            waiting.setdefault(PLAN["need"][p], []).append(own_total)
        if p == 0:
            first_total = own_total
            totals[0] = between(own_total, [(0, 1), (3, 2)])
        elif p == 1:
            totals[1] = between(own_total, [(0, 1), (3, 2), (1, 3), (2, 0)])
            relay = add(False, [first_total, totals[1]], [], [], PLAN["add"].get(3, 1), VMEM(part, F32), "add_relay")
            if 3 in PLAN["need"]:
                waiting.setdefault(PLAN["need"][3], []).append(relay)
            totals[3] = between(relay, [(1, 2), (2, 1)])
        else:
            totals[2] = between(own_total, [(0, 1), (1, 0), (2, 3), (3, 2)])

    in_vmem = pl.BlockSpec(memory_space=VMEM)
    terms = [mine, totals[2], totals[3], totals[1], *swapped]
    first_grad, second_grad = pl.pallas_call(
        last_kernel,
        out_shape=[jax.ShapeDtypeStruct(part[1:], F32)] * 2,
        in_specs=[pl.BlockSpec(memory_space=pltpu.SMEM)] + [in_vmem] * len(terms),
        out_specs=[in_vmem] * 2,
        compiler_params=pltpu.CompilerParams(vmem_limit_bytes=VMEM_LIMIT),
        cost_estimate=pl.CostEstimate(flops=PLAN["last"], bytes_accessed=1, transcendentals=0),
        name="add_last",
    )(info, *terms)
    returned = outs[groups - 1].reshape(1, 4, 1, pixels, channels)
    return (returned, first_grad[None, None], second_grad[None, None])


def solution(mesh):
    return jax.shard_map(
        on_device,
        mesh=mesh,
        in_specs=(
            P("section", None, "rep", None, None),
            P(None, None, "rep", None, None),
            P("section", None, None, None, None),
            P("section", None, None, None, None),
        ),
        out_specs=(
            P("section", None, "rep", None, None),
            P("section", None, None, "rep", None),
            P("section", None, None, "rep", None),
        ),
        check_vma=False,
    )
```
